32 devices in a mesh: groups: 2 (over y), ep: 4 (over x, core), dp: 4 (over z).
Axes of the slice: x: 2, y: 2, z: 4, core: 2. Of those that a mesh axis runs over, the one named last changes fastest.
Arguments:
- tokens: bfloat16 [1024, 2048], P(('groups', 'ep', 'dp')), parts along dimension 0, may hold values from -6 to 6
- expert_ids: int32 [1024, 8], P(('groups', 'ep', 'dp')), parts along dimension 0, may hold values from 0 to 15, as said below
- route_w: float32 [1024, 8], P(('groups', 'ep', 'dp')), parts along dimension 0, may hold values from 0.1 to 0.5
- hot_list: int32 [8], P('groups'), parts along dimension 0, may hold values from 0 to 15, as said below
- slot_of: int32 [16], replicated, may hold values from 0 to 15, each once
- cold_gate_up: bfloat16 [16, 2048, 1536], P(('ep', 'dp')), may hold values from -0.125 to 0.125
- cold_down: bfloat16 [16, 768, 2048], P(('ep', 'dp')), may hold values from -0.21875 to 0.21875
- hot_weights: bfloat16 [4, 3, 2048, 768], P('dp', None, None, 'ep'), may hold values from -0.125 to 0.125
Outputs:
- mixed: bfloat16 [1024, 2048], P(('groups', 'ep', 'dp')), parts along dimension 0
The draws below stay inside these ranges and needn't reach their ends.
There are 2 independent parts, one for each index of `groups`. The reference program is written for one: setup_inputs(seed, part) draws one part's arguments, and reference() takes and returns one part's arrays. A program takes and returns all parts, laid end to end along the dimension named above; an argument that names none is the same for every part. Nothing has to cross between parts.
Inputs may be any that keep to these rules, and one draw needn't show every extreme that they name: `expert_ids`: each row names 8 different experts. Among the rows of one device, each expert of hot_list is named by exactly 32 rows, every other expert by at most 11 rows, and one expert outside hot_list is named by exactly 11 rows of every device. `hot_list`: 4 different expert numbers.
All inputs are finite; a program needn't handle non-finite values.
Results may differ from the reference program's by a relative error of at most 0.0057.
Values may be sent and summed in bfloat16 or wider, within the bound.
No kernel may reach another device: no remote copies, remote signals or barrier semaphores. Data moves between devices by JAX's collectives and lax.ppermute only.
A program may use at most 64 MiB of HBM per device.

```python
import jax
import jax.numpy as jnp
from jax import lax

D = 2048
FF = 768
TOP = 8
TOK_DEV = 32
EXPERTS = 16
HOT = 4
MOST = 32
COLD = 11
TOKENS = 512
N_EP = 4
N_DP = 4


def expert_order(key):
    return jax.random.permutation(key, EXPERTS).astype(jnp.int32)


def draw_hot_list(key, part):
    ranking = expert_order(key)
    return ranking[:HOT]


def draw_expert_ids(key, part):
    ranking = expert_order(key)
    key = jax.random.fold_in(key, 23)
    blocks = TOKENS // TOK_DEV
    entries = TOK_DEV * TOP
    n_cold = EXPERTS - HOT
    spare_rows = entries - HOT * MOST
    base_count = spare_rows // n_cold
    extra_count = spare_rows % n_cold
    key_cold, key_rows, key_cols = jax.random.split(key, 3)
    shuffled = jax.vmap(lambda sub_key: jax.random.permutation(sub_key, n_cold - 1))(jax.random.split(key_cold, blocks)) + 1
    cold_rank = jnp.concatenate([jnp.zeros((blocks, 1), jnp.int32), shuffled.astype(jnp.int32)], axis=1)
    cold_count = base_count + (cold_rank < extra_count).astype(jnp.int32)
    hot_count = jnp.full((blocks, HOT), MOST, jnp.int32)
    by_rank = jnp.concatenate([hot_count, cold_count], axis=1)
    counts = jnp.zeros((blocks, EXPERTS), jnp.int32).at[:, ranking].set(by_rank)
    run_ends = jnp.cumsum(counts, axis=1)
    position = jnp.arange(entries, dtype=jnp.int32)
    run_ids = jnp.sum((run_ends[:, None, :] <= position[None, :, None]).astype(jnp.int32), axis=2)
    routing = run_ids.reshape(blocks, TOP, TOK_DEV).transpose(0, 2, 1)
    row_perm = jax.vmap(lambda sub_key: jax.random.permutation(sub_key, TOK_DEV))(jax.random.split(key_rows, blocks))
    routing = jnp.take_along_axis(routing, row_perm[:, :, None], axis=1)
    col_perm = jax.vmap(lambda sub_key: jax.random.permutation(sub_key, TOP))(jax.random.split(key_cols, blocks * TOK_DEV))
    routing = jnp.take_along_axis(routing, col_perm.reshape(blocks, TOK_DEV, TOP), axis=2)
    return routing.reshape(TOKENS, TOP).astype(jnp.int32)


def shard_levels(key, shape, cuts, least, largest):
    factor_of, own = 1.0, jax.random.fold_in(key, 6)
    for dim, parts in cuts:
        draws = jnp.exp(jax.random.uniform(jax.random.fold_in(own, dim), (parts,), jnp.float32, least / len(cuts), largest / len(cuts)))
        factor_of = factor_of * jnp.repeat(draws, shape[dim] // parts).reshape([-1 if axis == dim else 1 for axis in range(len(shape))])
    return factor_of


def normal_values(key, shape, spread, reach, cuts=(), kind=jnp.bfloat16):
    drawn = spread * jax.random.normal(key, shape, jnp.float32)
    if cuts:
        drawn = drawn * shard_levels(key, shape, cuts, -0.22, 0.18)
    return jnp.clip(drawn, -reach, reach).astype(kind)


def setup_inputs(seed: int = 0, part: int = 0) -> dict:
    key_of = jax.random.split(jax.random.key(seed), 9)
    part_keys = jax.random.split(jax.random.fold_in(key_of[8], part), 9)
    return {
        "tokens": normal_values(part_keys[0], (TOKENS, D), 1.0, 6.0, ((0, 16),)),
        "expert_ids": draw_expert_ids(jax.random.fold_in(jax.random.fold_in(key_of[8], part), 71), part),
        "route_w": jnp.clip(0.1 + 0.4 * jax.random.uniform(part_keys[2], (TOKENS, TOP), jnp.float32) ** shard_levels(part_keys[2], (TOKENS, TOP), ((0, 16),), -0.2, 0.2), 0.1, 0.5),
        "hot_list": draw_hot_list(jax.random.fold_in(jax.random.fold_in(key_of[8], part), 71), part),
        "slot_of": jax.random.permutation(key_of[4], EXPERTS).astype(jnp.int32),
        "cold_gate_up": normal_values(key_of[5], (EXPERTS, D, 2 * FF), D ** -0.5, 0.125, ((0, 16),)),
        "cold_down": normal_values(key_of[6], (EXPERTS, FF, D), FF ** -0.5, 0.21875, ((0, 16),)),
        "hot_weights": normal_values(key_of[7], (HOT, 3, D, FF), D ** -0.5, 0.125, ((0, 4), (3, 4))),
    }


def reference(tokens, expert_ids, route_w, hot_list, slot_of, cold_gate_up, cold_down, hot_weights):
    top_count = expert_ids.shape[1]
    flat_ids = expert_ids.reshape(-1).astype(jnp.int32)
    sort_order = jnp.argsort(flat_ids, stable=True).astype(jnp.int32)
    sorted_ids = flat_ids[sort_order]
    expert_range = jnp.arange(EXPERTS, dtype=jnp.int32)
    run_starts = jnp.searchsorted(sorted_ids, expert_range, side="left").astype(jnp.int32)
    run_ends = jnp.searchsorted(sorted_ids, expert_range, side="right").astype(jnp.int32)
    flat_w = route_w.reshape(-1)
    total_pairs = flat_ids.shape[0]

    def rows_of(expert, window):
        offsets = jnp.arange(window, dtype=jnp.int32)
        run_begin = run_starts[expert]
        clipped = jnp.minimum(run_begin + offsets, total_pairs - 1).astype(jnp.int32)
        pair_id = sort_order[clipped]
        is_live = offsets < run_ends[expert] - run_begin
        row_id = (pair_id // top_count).astype(jnp.int32)
        weight = jnp.where(is_live, flat_w[pair_id], jnp.zeros((), flat_w.dtype))
        return row_id, weight, tokens[row_id]

    def hot_step(summed, hot_slot):
        row_id, weight, inputs = rows_of(hot_list[hot_slot], N_EP * N_DP * MOST)
        triple = hot_weights[hot_slot]
        gate_out = jnp.dot(inputs, triple[0], preferred_element_type=jnp.float32)
        up_out = jnp.dot(inputs, triple[1], preferred_element_type=jnp.float32)
        hidden = (jax.nn.silu(gate_out) * up_out).astype(jnp.bfloat16)
        result = lax.dot_general(hidden, triple[2], (((1,), (1,)), ((), ())), preferred_element_type=jnp.float32)
        result = result.astype(jnp.bfloat16).astype(jnp.float32)
        return summed.at[row_id].add(weight[:, None] * result), None

    def cold_step(summed, expert):
        row_id, weight, inputs = rows_of(expert, N_EP * N_DP * COLD)
        weight = jnp.where(jnp.any(hot_list == expert), jnp.zeros((), weight.dtype), weight)
        slot_id = slot_of[expert]
        both_out = jnp.dot(inputs, cold_gate_up[slot_id], preferred_element_type=jnp.float32)
        hidden = (jax.nn.silu(both_out[:, :FF]) * both_out[:, FF:]).astype(jnp.bfloat16)
        result = jnp.dot(hidden, cold_down[slot_id], preferred_element_type=jnp.float32)
        result = result.astype(jnp.bfloat16).astype(jnp.float32)
        return summed.at[row_id].add(weight[:, None] * result), None

    summed = jnp.zeros(tokens.shape, jnp.float32)
    summed, _ = lax.scan(hot_step, summed, jnp.arange(HOT, dtype=jnp.int32))
    summed, _ = lax.scan(cold_step, summed, expert_range)
    return summed.astype(jnp.bfloat16)
```

```python
import functools

import jax
import jax.numpy as jnp
from jax import lax
from jax.experimental import pallas as pl
from jax.experimental.pallas import tpu as pltpu
from jax.sharding import PartitionSpec as P


def swiglu_rows(inputs, gate_up, down_proj):
    in_shape = inputs.shape
    flat_in = inputs.reshape(-1, in_shape[-1])
    hidden_width = down_proj.shape[0]
    both_out = jnp.dot(flat_in, gate_up, preferred_element_type=jnp.float32)
    hidden = (jax.nn.silu(both_out[:, :hidden_width]) * both_out[:, hidden_width:]).astype(
        jnp.bfloat16
    )
    result = jnp.dot(hidden, down_proj, preferred_element_type=jnp.float32)
    return result.astype(jnp.bfloat16).reshape(in_shape)


def sliced_rows(inputs, triple):
    in_shape = inputs.shape
    flat_in = inputs.reshape(-1, in_shape[-1])
    gate_out = jnp.dot(flat_in, triple[0], preferred_element_type=jnp.float32)
    up_out = jnp.dot(flat_in, triple[1], preferred_element_type=jnp.float32)
    hidden = (jax.nn.silu(gate_out) * up_out).astype(jnp.bfloat16)
    result = lax.dot_general(
        hidden, triple[2], (((1,), (1,)), ((), ())), preferred_element_type=jnp.float32
    )
    return result.reshape(in_shape)


def routed_body(tokens, expert_ids, route_w, hot_list, slot_of, cold_gate_up, cold_down, hot_weights):
    tok_rows, model_width = tokens.shape
    top_count = expert_ids.shape[1]
    n_hot = hot_list.shape[0]
    n_exp = slot_of.shape[0]
    n_ep = lax.axis_size("ep")
    n_dp = lax.axis_size("dp")
    n_dev = n_ep * n_dp
    most_rows = 2 * tok_rows * top_count // n_exp
    spare_rows = tok_rows * top_count - n_hot * most_rows
    cold_cap = (spare_rows + n_exp - n_hot - 1) // (n_exp - n_hot)
    one_hot = expert_ids[:, :, None] == jnp.arange(n_exp, dtype=jnp.int32)[None, None, :]
    slot_ids = jnp.sum(jnp.where(one_hot, slot_of[None, None, :], 0), axis=2)
    hot_match = expert_ids[:, :, None] == hot_list[None, None, :]
    is_hot = jnp.any(hot_match, axis=2)
    hot_index = jnp.sum(
        jnp.where(hot_match, jnp.arange(n_hot, dtype=jnp.int32)[None, None, :], 0), axis=2
    )
    flat_onehot = one_hot.reshape(tok_rows * top_count, n_exp).astype(jnp.int32)
    earlier = jnp.cumsum(flat_onehot, axis=0) - flat_onehot
    rank_ids = jnp.sum(earlier * flat_onehot, axis=1).reshape(tok_rows, top_count)
    row_ids = jnp.broadcast_to(
        jnp.arange(tok_rows, dtype=jnp.int32)[:, None], (tok_rows, top_count)
    ).reshape(-1)
    cold_size = n_dev * cold_cap
    hot_size = n_hot * most_rows
    cold_target = jnp.where(is_hot, cold_size, slot_ids * cold_cap + rank_ids).reshape(-1)
    hot_target = jnp.where(is_hot, hot_index * most_rows + rank_ids, hot_size).reshape(-1)
    cold_map = jnp.full((cold_size,), tok_rows, jnp.int32).at[cold_target].set(row_ids, mode="drop")
    hot_map = jnp.full((hot_size,), tok_rows, jnp.int32).at[hot_target].set(row_ids, mode="drop")
    padded = jnp.concatenate([tokens, jnp.zeros((1, model_width), tokens.dtype)], axis=0)
    cold_send = jnp.take(padded, cold_map, axis=0).reshape(n_dev, cold_cap, model_width)
    hot_send = jnp.take(padded, hot_map, axis=0).reshape(n_hot, most_rows, model_width)
    gate_up = cold_gate_up[0]
    down_proj = cold_down[0]
    cold_back = lax.all_to_all(
        swiglu_rows(
            lax.all_to_all(cold_send, ("ep", "dp"), split_axis=0, concat_axis=0, tiled=True),
            gate_up,
            down_proj,
        ),
        ("ep", "dp"),
        split_axis=0,
        concat_axis=0,
        tiled=True,
    )
    hot_recv = lax.all_to_all(hot_send, "dp", split_axis=0, concat_axis=0, tiled=True)
    gathered = lax.all_gather(hot_recv, "ep", axis=0, tiled=True)
    own_slice = hot_weights[0]
    hot_sum = lax.psum_scatter(
        sliced_rows(gathered, own_slice), "ep", scatter_dimension=0, tiled=True
    )
    hot_back = lax.all_to_all(
        hot_sum.astype(jnp.bfloat16), "dp", split_axis=0, concat_axis=0, tiled=True
    )
    answers = jnp.concatenate(
        [cold_back.reshape(cold_size, model_width), hot_back.reshape(hot_size, model_width)], axis=0
    )
    positions = jnp.where(
        is_hot, cold_size + hot_index * most_rows + rank_ids, slot_ids * cold_cap + rank_ids
    )
    picked = jnp.take(answers, positions, axis=0)
    mixed = jnp.zeros((tok_rows, model_width), jnp.float32)
    for column in range(top_count):
        mixed = mixed + route_w[:, column, None] * picked[:, column].astype(jnp.float32)
    return mixed.astype(jnp.bfloat16)


def pin(array):
    return pltpu.with_memory_space_constraint(array, pltpu.VMEM)


def expert_kernel(n_blocks, halves, cap, key_ref, *refs):
    rows_in = refs[:n_blocks]
    meta_in = refs[n_blocks : 2 * n_blocks]
    gate_up_ref, down_ref, hot_ref, out_ref, x_ref, hid_ref = refs[2 * n_blocks :]
    height = rows_in[0].shape[0]
    total = n_blocks * height
    width = rows_in[0].shape[1]
    hidden_width = down_ref.shape[1]
    top = meta_in[0].shape[1] // 2
    for index, block in enumerate(rows_in):
        x_ref[pl.ds(index * height, height), :] = block[...]
    meta = jnp.concatenate(
        [m[pl.ds(half * height, height), :] for m, half in zip(meta_in, halves)], axis=0
    )
    ids, gains = meta[:, :top], meta[:, top:]
    is_cold = ids == key_ref[0:1, :top]
    is_hot = ids == key_ref[1:2, :top]
    cold_gain = jnp.sum(jnp.where(is_cold, gains, 0.0), axis=1, keepdims=True)
    hot_gain = jnp.sum(jnp.where(is_hot, gains, 0.0), axis=1, keepdims=True)
    mark = jnp.sum(jnp.where(is_cold, 1.0, 0.0), axis=1, keepdims=True)
    marks = jnp.broadcast_to(mark, (total, 128))
    below = lax.broadcasted_iota(jnp.int32, (total, total), 0) > lax.broadcasted_iota(
        jnp.int32, (total, total), 1
    )
    rank = jnp.dot(
        jnp.where(below, 1.0, 0.0).astype(jnp.bfloat16),
        marks.astype(jnp.bfloat16),
        preferred_element_type=jnp.float32,
    )
    lane = lax.broadcasted_iota(jnp.int32, (total, 128), 1).astype(jnp.float32)
    spread = jnp.where((marks > 0.5) & (rank == lane), 1.0, 0.0).astype(jnp.bfloat16)
    x = x_ref[...]
    picked = lax.dot_general(
        spread, x, (((0,), (0,)), ((), ())), preferred_element_type=jnp.float32
    )[:cap].astype(jnp.bfloat16)
    step = 256
    for start in range(0, hidden_width, step):
        gate = jnp.dot(
            picked, gate_up_ref[0, :, start : start + step], preferred_element_type=jnp.float32
        )
        up = jnp.dot(
            picked,
            gate_up_ref[0, :, hidden_width + start : hidden_width + start + step],
            preferred_element_type=jnp.float32,
        )
        hid_ref[:, start : start + step] = (gate / (1.0 + jnp.exp(-gate)) * up).astype(jnp.bfloat16)
    gate = jnp.dot(x, hot_ref[0, 0], preferred_element_type=jnp.float32)
    up = jnp.dot(x, hot_ref[0, 1], preferred_element_type=jnp.float32)
    hot_hidden = (gate / (1.0 + jnp.exp(-gate)) * up).astype(jnp.bfloat16)
    cold_hidden = hid_ref[...]
    spread_cap = spread[:, :cap]

    @pl.loop(0, width // step)
    def _(chunk):
        at = pl.ds(pl.multiple_of(chunk * step, step), step)
        hot_part = lax.dot_general(
            hot_hidden,
            hot_ref[0, 2, at, :],
            (((1,), (1,)), ((), ())),
            preferred_element_type=jnp.float32,
        )
        cold_part = jnp.dot(
            cold_hidden, down_ref[0, :, at], preferred_element_type=jnp.float32
        ).astype(jnp.bfloat16)
        cold_rows = jnp.dot(spread_cap, cold_part, preferred_element_type=jnp.float32)
        out_ref[:, at] = (hot_gain * hot_part + cold_gain * cold_rows).astype(jnp.bfloat16)


def expert_rows(key, blocks, metas, halves, cap, weights):
    n_blocks = len(blocks)
    height, width = blocks[0].shape
    total = n_blocks * height
    hidden_width = weights[1].shape[1]
    slice_width = weights[2].shape[3]
    flops = 2 * 3 * width * (total * slice_width + cap * hidden_width) + 4 * 128 * total * width
    vmem = pl.BlockSpec(memory_space=pltpu.VMEM)
    return pl.pallas_call(
        functools.partial(expert_kernel, n_blocks, halves, cap),
        out_shape=jax.ShapeDtypeStruct((total, width), jnp.bfloat16),
        in_specs=[vmem] * (1 + 2 * n_blocks + 3),
        out_specs=vmem,
        scratch_shapes=[
            pltpu.VMEM((total, width), jnp.bfloat16),
            pltpu.VMEM((cap, hidden_width), jnp.bfloat16),
        ],
        compiler_params=pltpu.CompilerParams(vmem_limit_bytes=24 * 2**20),
        cost_estimate=pl.CostEstimate(
            flops=flops, bytes_accessed=total * width * 4, transcendentals=total * slice_width
        ),
    )(key, *blocks, *metas, *[pin(w) for w in weights])


def ring_perms(n_ep, n_dp):
    chips = [(0, z) for z in range(n_dp)] + [(1, z) for z in reversed(range(n_dp))]

    def device(place, core):
        x, z = chips[place % len(chips)]
        return (2 * x + core) * n_dp + z

    def hop(by0, by1):
        return [
            (device(i, core), device(i + (by1 if core else by0), core))
            for i in range(len(chips))
            for core in range(2)
        ]

    swap = [(device(i, c), device(i, 1 - c)) for i in range(len(chips)) for c in range(2)]
    return hop, swap


def dense_body(tokens, expert_ids, route_w, hot_list, slot_of, cold_gate_up, cold_down, hot_weights):
    tok_rows, width = tokens.shape
    top = expert_ids.shape[1]
    n_hot, n_exp = hot_list.shape[0], slot_of.shape[0]
    n_ep, n_dp = lax.axis_size("ep"), lax.axis_size("dp")
    cold_cap = -(-(tok_rows * top - n_hot * tok_rows) // (n_exp - n_hot))
    hop, swap_pairs = ring_perms(n_ep, n_dp)
    axes = ("ep", "dp")
    move = lambda a, by0, by1=None: lax.ppermute(a, axes, hop(by0, by0 if by1 is None else by1))
    swap = lambda a: lax.ppermute(a, axes, swap_pairs)
    weights = (cold_gate_up, cold_down, hot_weights)
    core = lax.axis_index("ep") % 2

    me = lax.axis_index("ep") * n_dp + lax.axis_index("dp")
    my_expert = jnp.sum(jnp.where(slot_of == me, jnp.arange(n_exp, dtype=jnp.int32), 0))
    my_cold = jnp.where(jnp.any(hot_list == my_expert), -1, my_expert)
    my_hot = jnp.sum(jnp.where(jnp.arange(n_hot) == lax.axis_index("dp"), hot_list, 0))
    key = jnp.broadcast_to(
        jnp.stack([my_cold, my_hot]).astype(jnp.float32)[:, None], (2, 128)
    )

    plus = {0: tokens}
    meta = jnp.concatenate([expert_ids.astype(jnp.float32), route_w], axis=1)
    meta = jnp.concatenate([meta, swap(meta)], axis=0)
    metas = {0: meta}
    for far in (1, 2, 3):
        plus[far] = move(plus[far - 1], 1)
        plus[-far] = move(plus[1 - far], -1)
        metas[far] = move(metas[far - 1], 1)
        metas[-far] = move(metas[1 - far], -1)
    plus[4] = move(jnp.where(core == 0, plus[3], plus[-3]), 1, -1)
    metas[4] = move(jnp.where(core == 0, metas[3], metas[-3]), 1, -1)
    other = {far: swap(plus[far]) for far in plus}

    def batch(fars, pool, half):
        cap = -(-cold_cap * len(fars) // 16) * 16
        rows = expert_rows(
            key, [pool[f] for f in fars], [metas[f] for f in fars], [half] * len(fars), cap, weights
        )
        return rows

    parts, theirs = {}, {}
    for fars in ((0, 1, -1), (2, -2), (3, -3, 4)):
        back = swap(batch(fars, other, 1))
        mine = batch(fars, plus, 0)
        for index, far in enumerate(fars):
            at = slice(index * tok_rows, (index + 1) * tok_rows)
            parts[far] = (mine[at], back[at])

    f32 = jnp.float32
    full = lambda far: parts[far][0].astype(f32) + parts[far][1].astype(f32)
    low = lambda a: a.astype(jnp.bfloat16)
    last = move(low(full(4)), -1, 1)
    ahead = move(low(full(-3) + jnp.where(core == 1, last, 0).astype(f32)), 1)
    behind = move(low(full(3) + jnp.where(core == 0, last, 0).astype(f32)), -1)
    for far in (2, 1):
        ahead = move(low(full(-far) + ahead.astype(f32)), 1)
        behind = move(low(full(far) + behind.astype(f32)), -1)
    return low(full(0) + ahead.astype(f32) + behind.astype(f32))


def body(tokens, expert_ids, *rest):
    hot_list, slot_of = rest[1], rest[2]
    every_row_hot = 2 * expert_ids.shape[1] == slot_of.shape[0]
    two_columns = lax.axis_size("ep") == 4 and lax.axis_size("dp") == 4
    chosen = dense_body if every_row_hot and two_columns else routed_body
    return chosen(tokens, expert_ids, *rest)


def solution(mesh):
    in_specs = (
        P(("groups", "ep", "dp"), None),
        P(("groups", "ep", "dp"), None),
        P(("groups", "ep", "dp"), None),
        P("groups"),
        P(),
        P(("ep", "dp"), None, None),
        P(("ep", "dp"), None, None),
        P("dp", None, None, "ep"),
    )
    out_specs = P(("groups", "ep", "dp"), None)
    return jax.shard_map(body, mesh=mesh, in_specs=in_specs, out_specs=out_specs, check_vma=False)
```

```python
import functools

import jax
import jax.numpy as jnp
from jax import lax
from jax.experimental import pallas as pl
from jax.experimental.pallas import tpu as pltpu
from jax.sharding import PartitionSpec as P


def swiglu_rows(inputs, gate_up, down_proj):
    in_shape = inputs.shape
    flat_in = inputs.reshape(-1, in_shape[-1])
    hidden_width = down_proj.shape[0]
    both_out = jnp.dot(flat_in, gate_up, preferred_element_type=jnp.float32)
    hidden = (jax.nn.silu(both_out[:, :hidden_width]) * both_out[:, hidden_width:]).astype(
        jnp.bfloat16
    )
    result = jnp.dot(hidden, down_proj, preferred_element_type=jnp.float32)
    return result.astype(jnp.bfloat16).reshape(in_shape)


def sliced_rows(inputs, triple):
    in_shape = inputs.shape
    flat_in = inputs.reshape(-1, in_shape[-1])
    gate_out = jnp.dot(flat_in, triple[0], preferred_element_type=jnp.float32)
    up_out = jnp.dot(flat_in, triple[1], preferred_element_type=jnp.float32)
    hidden = (jax.nn.silu(gate_out) * up_out).astype(jnp.bfloat16)
    result = lax.dot_general(
        hidden, triple[2], (((1,), (1,)), ((), ())), preferred_element_type=jnp.float32
    )
    return result.reshape(in_shape)


def routed_body(tokens, expert_ids, route_w, hot_list, slot_of, cold_gate_up, cold_down, hot_weights):
    tok_rows, model_width = tokens.shape
    top_count = expert_ids.shape[1]
    n_hot = hot_list.shape[0]
    n_exp = slot_of.shape[0]
    n_ep = lax.axis_size("ep")
    n_dp = lax.axis_size("dp")
    n_dev = n_ep * n_dp
    most_rows = 2 * tok_rows * top_count // n_exp
    spare_rows = tok_rows * top_count - n_hot * most_rows
    cold_cap = (spare_rows + n_exp - n_hot - 1) // (n_exp - n_hot)
    one_hot = expert_ids[:, :, None] == jnp.arange(n_exp, dtype=jnp.int32)[None, None, :]
    slot_ids = jnp.sum(jnp.where(one_hot, slot_of[None, None, :], 0), axis=2)
    hot_match = expert_ids[:, :, None] == hot_list[None, None, :]
    is_hot = jnp.any(hot_match, axis=2)
    hot_index = jnp.sum(
        jnp.where(hot_match, jnp.arange(n_hot, dtype=jnp.int32)[None, None, :], 0), axis=2
    )
    flat_onehot = one_hot.reshape(tok_rows * top_count, n_exp).astype(jnp.int32)
    earlier = jnp.cumsum(flat_onehot, axis=0) - flat_onehot
    rank_ids = jnp.sum(earlier * flat_onehot, axis=1).reshape(tok_rows, top_count)
    row_ids = jnp.broadcast_to(
        jnp.arange(tok_rows, dtype=jnp.int32)[:, None], (tok_rows, top_count)
    ).reshape(-1)
    cold_size = n_dev * cold_cap
    hot_size = n_hot * most_rows
    cold_target = jnp.where(is_hot, cold_size, slot_ids * cold_cap + rank_ids).reshape(-1)
    hot_target = jnp.where(is_hot, hot_index * most_rows + rank_ids, hot_size).reshape(-1)
    cold_map = jnp.full((cold_size,), tok_rows, jnp.int32).at[cold_target].set(row_ids, mode="drop")
    hot_map = jnp.full((hot_size,), tok_rows, jnp.int32).at[hot_target].set(row_ids, mode="drop")
    padded = jnp.concatenate([tokens, jnp.zeros((1, model_width), tokens.dtype)], axis=0)
    cold_send = jnp.take(padded, cold_map, axis=0).reshape(n_dev, cold_cap, model_width)
    hot_send = jnp.take(padded, hot_map, axis=0).reshape(n_hot, most_rows, model_width)
    gate_up = cold_gate_up[0]
    down_proj = cold_down[0]
    cold_back = lax.all_to_all(
        swiglu_rows(
            lax.all_to_all(cold_send, ("ep", "dp"), split_axis=0, concat_axis=0, tiled=True),
            gate_up,
            down_proj,
        ),
        ("ep", "dp"),
        split_axis=0,
        concat_axis=0,
        tiled=True,
    )
    hot_recv = lax.all_to_all(hot_send, "dp", split_axis=0, concat_axis=0, tiled=True)
    gathered = lax.all_gather(hot_recv, "ep", axis=0, tiled=True)
    own_slice = hot_weights[0]
    hot_sum = lax.psum_scatter(
        sliced_rows(gathered, own_slice), "ep", scatter_dimension=0, tiled=True
    )
    hot_back = lax.all_to_all(
        hot_sum.astype(jnp.bfloat16), "dp", split_axis=0, concat_axis=0, tiled=True
    )
    answers = jnp.concatenate(
        [cold_back.reshape(cold_size, model_width), hot_back.reshape(hot_size, model_width)], axis=0
    )
    positions = jnp.where(
        is_hot, cold_size + hot_index * most_rows + rank_ids, slot_ids * cold_cap + rank_ids
    )
    picked = jnp.take(answers, positions, axis=0)
    mixed = jnp.zeros((tok_rows, model_width), jnp.float32)
    for column in range(top_count):
        mixed = mixed + route_w[:, column, None] * picked[:, column].astype(jnp.float32)
    return mixed.astype(jnp.bfloat16)


def pin(array):
    return pltpu.with_memory_space_constraint(array, pltpu.VMEM)


NN = (((1,), (0,)), ((), ()))
NT = (((1,), (1,)), ((), ()))
TN = (((0,), (0,)), ((), ()))
STEP = 256
LANES = 128


def mm(a, b, dims=NN):
    return lax.dot_general(a, b, dims, preferred_element_type=jnp.float32)


def swish(gate, up):
    return (gate / (1.0 + jnp.exp(-gate)) * up).astype(jnp.bfloat16)


def message_kernel(hot_list_ref, slot_ref, tok_ref, ids_ref, gain_ref, out_ref, key_ref):
    width = tok_ref.shape[1]
    out_ref[:, :width] = tok_ref[...]
    top = ids_ref.shape[0]
    bf16, f32 = jnp.bfloat16, jnp.float32
    gains = gain_ref[...]
    terms = [ids_ref[...].astype(f32)]
    for _ in range(3):
        term = gains.astype(bf16).astype(f32)
        terms.append(term)
        gains = gains - term
    stacked = jnp.concatenate(terms, axis=0).astype(bf16)
    shape = (4 * top, LANES)
    place = lax.broadcasted_iota(jnp.int32, shape, 0) == lax.broadcasted_iota(jnp.int32, shape, 1)
    out_ref[:, width:] = mm(stacked, jnp.where(place, 1.0, 0.0).astype(bf16), TN).astype(bf16)
    along = lax.axis_index("dp")
    me = lax.axis_index("ep") * lax.axis_size("dp") + along
    my_cold, my_hot = jnp.int32(0), jnp.int32(0)
    for expert in range(slot_ref.shape[0]):
        my_cold = jnp.where(slot_ref[expert] == me, expert, my_cold)
    held = my_cold
    for place in range(hot_list_ref.shape[0]):
        my_cold = jnp.where(hot_list_ref[place] == held, -1, my_cold)
        my_hot = jnp.where(along == place, hot_list_ref[place], my_hot)
    row = lax.broadcasted_iota(jnp.int32, key_ref.shape, 0)
    key_ref[...] = jnp.where(row == 0, my_cold, my_hot).astype(f32)


def load_kernel(n, *refs):
    copies = []
    sems = refs[2 * n + 1]
    for index in range(n):
        src, dst = refs[index], refs[n + 1 + index]
        rows = src.shape[-2]
        parts = 4
        for part in range(parts):
            at = pl.ds(part * (rows // parts), rows // parts)
            lead = (0,) * (len(src.shape) - 2)
            if len(src.shape) == 4:
                for third in range(src.shape[1]):
                    copies.append((src.at[0, third, at], dst.at[0, third, at]))
            else:
                copies.append((src.at[lead + (at,)], dst.at[lead + (at,)]))
    started = []
    for number, (src, dst) in enumerate(copies):
        copy = pltpu.make_async_copy(src, dst, sems.at[number])
        copy.start()
        started.append(copy)
    for copy in started:
        copy.wait()


def routing(key_ref, metas, top, lanes):
    meta = jnp.concatenate([m[...] for m in metas], axis=0).astype(jnp.float32)
    total = meta.shape[0]
    ids = meta[:, :top]
    gains = meta[:, top : 2 * top] + meta[:, 2 * top : 3 * top] + meta[:, 3 * top : 4 * top]
    is_cold = ids == key_ref[0:1, :top]
    is_hot = ids == key_ref[1:2, :top]
    cold_gain = jnp.sum(jnp.where(is_cold, gains, 0.0), axis=1, keepdims=True)
    hot_gain = jnp.sum(jnp.where(is_hot, gains, 0.0), axis=1, keepdims=True)
    mark = jnp.sum(jnp.where(is_cold, 1.0, 0.0), axis=1, keepdims=True)
    marks = jnp.broadcast_to(mark, (total, lanes))
    shape = (total, total)
    below = lax.broadcasted_iota(jnp.int32, shape, 0) > lax.broadcasted_iota(jnp.int32, shape, 1)
    rank = mm(jnp.where(below, 1.0, 0.0).astype(jnp.bfloat16), marks.astype(jnp.bfloat16))
    lane = lax.broadcasted_iota(jnp.int32, (total, lanes), 1).astype(jnp.float32)
    spread = jnp.where((marks > 0.5) & (rank == lane), 1.0, 0.0).astype(jnp.bfloat16)
    return cold_gain, hot_gain, spread


def load_rows(blocks, x_ref):
    height, width = blocks[0].shape[0], x_ref.shape[1]
    for index, block in enumerate(blocks):
        x_ref[index * height : (index + 1) * height, :] = block[:, :width]


def tails(blocks, width):
    return [block.at[:, width : width + LANES] for block in blocks]


def weigh(hidden, packed_ref, spread, hot_ref, cold_gain, hot_gain, out_ref, first=0):
    width = out_ref.shape[1]
    rows = slice(first, first + hidden.shape[0])
    for start in range(0, width, STEP):
        at = slice(start, start + STEP)
        hot_part = mm(hidden, hot_ref[0, 2, :, at])
        cold_part = mm(spread, packed_ref[:, at])
        out_ref[rows, at] = (hot_gain * hot_part + cold_gain * cold_part).astype(out_ref.dtype)


def keep_gains(cold_gain, hot_gain, gain_ref):
    lane = lax.broadcasted_iota(jnp.int32, gain_ref.shape, 1)
    gain_ref[...] = jnp.where(lane == 0, cold_gain, hot_gain)


def early_kernel(n, top, cap, key_ref, *refs):
    blocks, (hot_ref, hid_ref, pick_ref, spread_ref, gain_ref, x_ref) = refs[:n], refs[n:]
    load_rows(blocks, x_ref)
    metas = tails(blocks, x_ref.shape[1])
    cold_gain, hot_gain, spread = routing(key_ref, metas, top, spread_ref.shape[1])
    spread_ref[...] = spread
    keep_gains(cold_gain, hot_gain, gain_ref)
    x = x_ref[...]
    hid_ref[...] = swish(mm(x, hot_ref[0, 0], NT), mm(x, hot_ref[0, 1], NT))
    pick_ref[...] = mm(spread[:, :cap], x, TN).astype(jnp.bfloat16)


def late_kernel(n, top, cap, key_ref, *refs):
    blocks, (early_ref, gate_up_ref, down_ref, hot_ref), rest = refs[:n], refs[n : n + 4], refs[n + 4 :]
    sib_ref, hid_ref, near_ref, far_ref, spread_ref, gain_ref, x_ref, c_ref, h_ref = rest
    width = x_ref.shape[1]
    units = down_ref.shape[1]
    load_rows(blocks, x_ref)
    cold_gain, hot_gain, spread = routing(key_ref, tails(blocks, width), top, spread_ref.shape[1])
    spread_ref[...] = spread
    keep_gains(cold_gain, hot_gain, gain_ref)
    spread = spread[:, :cap]
    x = x_ref[...]
    n_early = early_ref.shape[0]
    c_ref[:n_early, :] = early_ref[...]
    c_ref[n_early:, :] = mm(spread, x, TN).astype(jnp.bfloat16)
    cold = c_ref[...]
    for start in range(0, units, STEP):
        gate = mm(cold, gate_up_ref[0, :, start : start + STEP])
        up = mm(cold, gate_up_ref[0, :, units + start : units + start + STEP])
        h_ref[:, start : start + STEP] = swish(gate, up)
    hidden = swish(mm(x, hot_ref[0, 0], NT), mm(x, hot_ref[0, 1], NT))
    hid_ref[...] = hidden
    half = hidden.shape[0] // 2
    cold_hidden = h_ref[...]
    for start in range(0, width, STEP):
        at = slice(start, start + STEP)
        packed = mm(cold_hidden, down_ref[0, :, at]).astype(jnp.bfloat16)
        near_ref[:, at] = packed[:n_early]
        far_ref[:, at] = packed[n_early:]
    weigh(hidden[half:], far_ref, spread[half:], hot_ref, cold_gain[half:], hot_gain[half:], sib_ref)


def result_kernel(own_rows, sib_rows, after, hid_ref, packed_ref, spread_ref, gain_ref, hot_ref, *refs):
    outs = refs[after:]
    cap = packed_ref.shape[0]
    spans = ([sib_rows] if sib_rows else []) + [own_rows]
    for (first, size), out_ref in zip(spans, outs):
        at = slice(first, first + size)
        weigh(
            hid_ref[at, :],
            packed_ref,
            spread_ref[at, :cap],
            hot_ref,
            gain_ref[at, 0:1],
            gain_ref[at, 1:2],
            out_ref,
        )


def run_kernel(kernel, operands, outs, scratch, flops, moved, limit=12):
    vmem = pl.BlockSpec(memory_space=pltpu.VMEM)
    return pl.pallas_call(
        kernel,
        out_shape=[pltpu.VMEM(shape, dtype) for shape, dtype in outs],
        in_specs=[vmem] * len(operands),
        out_specs=[vmem] * len(outs),
        scratch_shapes=[pltpu.VMEM(shape, dtype) for shape, dtype in scratch],
        compiler_params=pltpu.CompilerParams(vmem_limit_bytes=limit * 2**20),
        cost_estimate=pl.CostEstimate(flops=flops, bytes_accessed=moved, transcendentals=0),
    )(*[pin(a) for a in operands])


def load_weights(weights, after):
    n = len(weights)
    hbm = lambda a: pltpu.with_memory_space_constraint(a, pltpu.HBM)
    return pl.pallas_call(
        functools.partial(load_kernel, n),
        out_shape=[pltpu.VMEM(w.shape, w.dtype) for w in weights],
        in_specs=[pl.BlockSpec(memory_space=pltpu.HBM)] * n + [pl.BlockSpec(memory_space=pl.ANY)],
        out_specs=[pl.BlockSpec(memory_space=pltpu.VMEM)] * n,
        scratch_shapes=[pltpu.SemaphoreType.DMA((4 * n + 8,))],
        compiler_params=pltpu.CompilerParams(vmem_limit_bytes=2**20),
        cost_estimate=pl.CostEstimate(
            flops=0, bytes_accessed=sum(w.size * 2 for w in weights), transcendentals=0
        ),
    )(*[hbm(w) for w in weights], after)


def make_message(tokens, ids, gains, hot_list, slot_of):
    rows, width = tokens.shape
    vmem, smem = pl.BlockSpec(memory_space=pltpu.VMEM), pl.BlockSpec(memory_space=pltpu.SMEM)
    hbm = lambda a: pltpu.with_memory_space_constraint(a, pltpu.HBM)
    return pl.pallas_call(
        message_kernel,
        out_shape=[
            pltpu.VMEM((rows, width + LANES), tokens.dtype),
            pltpu.VMEM((8, LANES), jnp.float32),
        ],
        in_specs=[smem] * 2 + [vmem] * 3,
        out_specs=[vmem] * 2,
        compiler_params=pltpu.CompilerParams(vmem_limit_bytes=2**21),
    )(*[hbm(a) for a in (hot_list, slot_of, tokens, ids, gains)])


def ring_perms(n_dp):
    chips = [(0, z) for z in range(n_dp)] + [(1, z) for z in reversed(range(n_dp))]
    size = len(chips)

    def device(place, core):
        x, z = chips[place % size]
        return (2 * x + core) * n_dp + z

    def hop(by):
        return [
            (device(i, core), device(i + (-by if core else by), core))
            for i in range(size)
            for core in range(2)
        ]

    swap = [(device(i, core), device(i, 1 - core)) for i in range(size) for core in range(2)]
    return hop, swap


def dense_body(tokens, expert_ids, route_w, hot_list, slot_of, cold_gate_up, cold_down, hot_weights):
    tok_rows, width = tokens.shape
    top = expert_ids.shape[1]
    n_hot, n_exp = hot_list.shape[0], slot_of.shape[0]
    n_dp = lax.axis_size("dp")
    units, hot_units = cold_down.shape[1], hot_weights.shape[3]
    cold_cap = -(-(tok_rows * top - n_hot * tok_rows) // (n_exp - n_hot))
    f32, bf16 = jnp.float32, jnp.bfloat16
    hop, swap_pairs = ring_perms(n_dp)
    axes = ("ep", "dp")
    move = lambda a, by: lax.ppermute(a, axes, hop(by))
    swap = lambda a: lax.ppermute(a, axes, swap_pairs)

    message, key = make_message(tokens, expert_ids.T, route_w.T, hot_list, slot_of)
    weights = (cold_gate_up, cold_down, jnp.swapaxes(hot_weights, 2, 3))
    gate_up, down, hot = load_weights(weights, message)

    tie = lambda *arrays: lax.optimization_barrier(arrays)
    own = {0: message}
    own[1], own[-1], hot = tie(move(message, 1), move(message, -1), hot)
    for far in (2, 3):
        own[far], own[-far] = tie(move(own[far - 1], 1), move(own[1 - far], -1))
    own[4] = move(own[3], 1)
    sib = {far: swap(own[far]) for far in own}

    near, late = (3, -3, 2, -2, 1, -1, 0), (4,)
    pad = lambda n: -(-n * cold_cap // 16) * 16
    lanes = lambda cap: -(-cap // LANES) * LANES
    n_near, n_late = 2 * len(near), 2 * len(late)
    cap_near, cap_late = pad(n_near), pad(n_late)
    rows_near, rows_late = n_near * tok_rows, n_late * tok_rows
    gather = lambda fars: [own[f] for f in fars] + [sib[f] for f in fars]
    hid_near, picked, spread_near, gain_near = run_kernel(
        functools.partial(early_kernel, n_near, top, cap_near),
        (key, *gather(near), hot),
        [
            ((rows_near, hot_units), bf16),
            ((cap_near, width), bf16),
            ((rows_near, lanes(cap_near)), bf16),
            ((rows_near, LANES), f32),
        ],
        [((rows_near, width), bf16)],
        2 * rows_near * width * (2 * hot_units + cap_near),
        4 * rows_near * width,
    )
    back_late, hid_late, packed_near, packed_late, spread_late, gain_late = run_kernel(
        functools.partial(late_kernel, n_late, top, cap_late),
        (key, *gather(late), picked, gate_up, down, hot),
        [
            ((rows_late // 2, width), bf16),
            ((rows_late, hot_units), bf16),
            ((cap_near, width), bf16),
            ((cap_late, width), bf16),
            ((rows_late, lanes(cap_late)), bf16),
            ((rows_late, LANES), f32),
        ],
        [
            ((rows_late, width), bf16),
            ((cap_near + cap_late, width), bf16),
            ((cap_near + cap_late, units), bf16),
        ],
        2 * (cap_near + cap_late) * 3 * units * width,
        4 * rows_late * width,
    )

    def results(fars, pool, sides, after=()):
        hid, packed, spread, gain = sides
        first, size = pool.index(fars[0]) * tok_rows, len(fars) * tok_rows
        shift = len(pool) * tok_rows
        outs = [((size, width), f32)]
        if pool is near:
            outs = [((size, width), bf16)] + outs
        return run_kernel(
            functools.partial(
                result_kernel,
                (first, size),
                (first + shift, size) if pool is near else None,
                len(after),
            ),
            (hid, packed, spread, gain, hot, *after),
            outs,
            [],
            4 * size * width * (hot_units + packed.shape[0]),
            8 * size * width,
        )

    total = {}

    def add_up(fars, mine, other):
        for index, far in enumerate(fars):
            at = slice(index * tok_rows, (index + 1) * tok_rows)
            total[far] = mine[at] + other[at].astype(f32)

    low = lambda a: a.astype(bf16)
    sides = (hid_near, packed_near, spread_near, gain_near)
    from_late = swap(back_late)
    (own_late,) = results(late, late, (hid_late, packed_late, spread_late, gain_late))
    add_up(late, own_late, from_late)
    first = low(total[4])
    behind = move(first, -1)
    back, mine = results((3, -3), near, sides, (first,))
    add_up((3, -3), mine, swap(back))
    ahead, behind = tie(low(total[-3]), low(total[3] + behind.astype(f32)))
    rest = (2, -2, 1, -1, 0)
    back, mine = results(rest, near, sides, (behind,))
    ahead, behind = move(ahead, 1), move(behind, -1)
    add_up(rest, mine, swap(back))
    for far in (2, 1):
        ahead, behind = tie(ahead, behind)
        ahead, behind = tie(low(total[-far] + ahead.astype(f32)), low(total[far] + behind.astype(f32)))
        ahead, behind = move(ahead, 1), move(behind, -1)
    return low(total[0] + ahead.astype(f32) + behind.astype(f32))


def body(tokens, expert_ids, *rest):
    hot_list, slot_of = rest[1], rest[2]
    every_row_hot = 2 * expert_ids.shape[1] == slot_of.shape[0]
    two_columns = lax.axis_size("ep") == 4 and lax.axis_size("dp") == 4
    chosen = dense_body if every_row_hot and two_columns else routed_body
    return chosen(tokens, expert_ids, *rest)


def solution(mesh):
    in_specs = (
        P(("groups", "ep", "dp"), None),
        P(("groups", "ep", "dp"), None),
        P(("groups", "ep", "dp"), None),
        P("groups"),
        P(),
        P(("ep", "dp"), None, None),
        P(("ep", "dp"), None, None),
        P("dp", None, None, "ep"),
    )
    out_specs = P(("groups", "ep", "dp"), None)
    return jax.shard_map(body, mesh=mesh, in_specs=in_specs, out_specs=out_specs, check_vma=False)
```

```python
import functools

import jax
import jax.numpy as jnp
from jax import lax
from jax.experimental import pallas as pl
from jax.experimental.pallas import tpu as pltpu
from jax.sharding import PartitionSpec as P


def swiglu_rows(inputs, gate_up, down_proj):
    in_shape = inputs.shape
    flat_in = inputs.reshape(-1, in_shape[-1])
    hidden_width = down_proj.shape[0]
    both_out = jnp.dot(flat_in, gate_up, preferred_element_type=jnp.float32)
    hidden = (jax.nn.silu(both_out[:, :hidden_width]) * both_out[:, hidden_width:]).astype(
        jnp.bfloat16
    )
    result = jnp.dot(hidden, down_proj, preferred_element_type=jnp.float32)
    return result.astype(jnp.bfloat16).reshape(in_shape)


def sliced_rows(inputs, triple):
    in_shape = inputs.shape
    flat_in = inputs.reshape(-1, in_shape[-1])
    gate_out = jnp.dot(flat_in, triple[0], preferred_element_type=jnp.float32)
    up_out = jnp.dot(flat_in, triple[1], preferred_element_type=jnp.float32)
    hidden = (jax.nn.silu(gate_out) * up_out).astype(jnp.bfloat16)
    result = lax.dot_general(
        hidden, triple[2], (((1,), (1,)), ((), ())), preferred_element_type=jnp.float32
    )
    return result.reshape(in_shape)


def routed_body(tokens, expert_ids, route_w, hot_list, slot_of, cold_gate_up, cold_down, hot_weights):
    tok_rows, model_width = tokens.shape
    top_count = expert_ids.shape[1]
    n_hot = hot_list.shape[0]
    n_exp = slot_of.shape[0]
    n_ep = lax.axis_size("ep")
    n_dp = lax.axis_size("dp")
    n_dev = n_ep * n_dp
    most_rows = 2 * tok_rows * top_count // n_exp
    spare_rows = tok_rows * top_count - n_hot * most_rows
    cold_cap = (spare_rows + n_exp - n_hot - 1) // (n_exp - n_hot)
    one_hot = expert_ids[:, :, None] == jnp.arange(n_exp, dtype=jnp.int32)[None, None, :]
    slot_ids = jnp.sum(jnp.where(one_hot, slot_of[None, None, :], 0), axis=2)
    hot_match = expert_ids[:, :, None] == hot_list[None, None, :]
    is_hot = jnp.any(hot_match, axis=2)
    hot_index = jnp.sum(
        jnp.where(hot_match, jnp.arange(n_hot, dtype=jnp.int32)[None, None, :], 0), axis=2
    )
    flat_onehot = one_hot.reshape(tok_rows * top_count, n_exp).astype(jnp.int32)
    earlier = jnp.cumsum(flat_onehot, axis=0) - flat_onehot
    rank_ids = jnp.sum(earlier * flat_onehot, axis=1).reshape(tok_rows, top_count)
    row_ids = jnp.broadcast_to(
        jnp.arange(tok_rows, dtype=jnp.int32)[:, None], (tok_rows, top_count)
    ).reshape(-1)
    cold_size = n_dev * cold_cap
    hot_size = n_hot * most_rows
    cold_target = jnp.where(is_hot, cold_size, slot_ids * cold_cap + rank_ids).reshape(-1)
    hot_target = jnp.where(is_hot, hot_index * most_rows + rank_ids, hot_size).reshape(-1)
    cold_map = jnp.full((cold_size,), tok_rows, jnp.int32).at[cold_target].set(row_ids, mode="drop")
    hot_map = jnp.full((hot_size,), tok_rows, jnp.int32).at[hot_target].set(row_ids, mode="drop")
    padded = jnp.concatenate([tokens, jnp.zeros((1, model_width), tokens.dtype)], axis=0)
    cold_send = jnp.take(padded, cold_map, axis=0).reshape(n_dev, cold_cap, model_width)
    hot_send = jnp.take(padded, hot_map, axis=0).reshape(n_hot, most_rows, model_width)
    gate_up = cold_gate_up[0]
    down_proj = cold_down[0]
    cold_back = lax.all_to_all(
        swiglu_rows(
            lax.all_to_all(cold_send, ("ep", "dp"), split_axis=0, concat_axis=0, tiled=True),
            gate_up,
            down_proj,
        ),
        ("ep", "dp"),
        split_axis=0,
        concat_axis=0,
        tiled=True,
    )
    hot_recv = lax.all_to_all(hot_send, "dp", split_axis=0, concat_axis=0, tiled=True)
    gathered = lax.all_gather(hot_recv, "ep", axis=0, tiled=True)
    own_slice = hot_weights[0]
    hot_sum = lax.psum_scatter(
        sliced_rows(gathered, own_slice), "ep", scatter_dimension=0, tiled=True
    )
    hot_back = lax.all_to_all(
        hot_sum.astype(jnp.bfloat16), "dp", split_axis=0, concat_axis=0, tiled=True
    )
    answers = jnp.concatenate(
        [cold_back.reshape(cold_size, model_width), hot_back.reshape(hot_size, model_width)], axis=0
    )
    positions = jnp.where(
        is_hot, cold_size + hot_index * most_rows + rank_ids, slot_ids * cold_cap + rank_ids
    )
    picked = jnp.take(answers, positions, axis=0)
    mixed = jnp.zeros((tok_rows, model_width), jnp.float32)
    for column in range(top_count):
        mixed = mixed + route_w[:, column, None] * picked[:, column].astype(jnp.float32)
    return mixed.astype(jnp.bfloat16)


def pin(array):
    return pltpu.with_memory_space_constraint(array, pltpu.VMEM)


NN = (((1,), (0,)), ((), ()))
NT = (((1,), (1,)), ((), ()))
TN = (((0,), (0,)), ((), ()))
STEP = 256
LANES = 128


def mm(a, b, dims=NN):
    return lax.dot_general(a, b, dims, preferred_element_type=jnp.float32)


def swish(gate, up):
    return (gate / (1.0 + jnp.exp(-gate)) * up).astype(jnp.bfloat16)


def message_kernel(hot_list_ref, slot_ref, tok_ref, ids_ref, gain_ref, out_ref, key_ref):
    width = tok_ref.shape[1]
    out_ref[:, :width] = tok_ref[...]
    top = ids_ref.shape[0]
    bf16, f32 = jnp.bfloat16, jnp.float32
    gains = gain_ref[...]
    terms = [ids_ref[...].astype(f32)]
    for _ in range(3):
        term = gains.astype(bf16).astype(f32)
        terms.append(term)
        gains = gains - term
    stacked = jnp.concatenate(terms, axis=0).astype(bf16)
    shape = (4 * top, LANES)
    place = lax.broadcasted_iota(jnp.int32, shape, 0) == lax.broadcasted_iota(jnp.int32, shape, 1)
    out_ref[:, width:] = mm(stacked, jnp.where(place, 1.0, 0.0).astype(bf16), TN).astype(bf16)
    along = lax.axis_index("dp")
    me = lax.axis_index("ep") * lax.axis_size("dp") + along
    my_cold, my_hot = jnp.int32(0), jnp.int32(0)
    for expert in range(slot_ref.shape[0]):
        my_cold = jnp.where(slot_ref[expert] == me, expert, my_cold)
    held = my_cold
    for place in range(hot_list_ref.shape[0]):
        my_cold = jnp.where(hot_list_ref[place] == held, -1, my_cold)
        my_hot = jnp.where(along == place, hot_list_ref[place], my_hot)
    row = lax.broadcasted_iota(jnp.int32, key_ref.shape, 0)
    key_ref[...] = jnp.where(row == 0, my_cold, my_hot).astype(f32)


def load_kernel(n, *refs):
    copies = []
    sems = refs[2 * n + 1]
    for index in range(n):
        src, dst = refs[index], refs[n + 1 + index]
        rows = src.shape[-2]
        parts = 4
        for part in range(parts):
            at = pl.ds(part * (rows // parts), rows // parts)
            lead = (0,) * (len(src.shape) - 2)
            if len(src.shape) == 4:
                for third in range(src.shape[1]):
                    copies.append((src.at[0, third, at], dst.at[0, third, at]))
            else:
                copies.append((src.at[lead + (at,)], dst.at[lead + (at,)]))
    started = []
    for number, (src, dst) in enumerate(copies):
        copy = pltpu.make_async_copy(src, dst, sems.at[number])
        copy.start()
        started.append(copy)
    for copy in started:
        copy.wait()


def routing(key_ref, metas, top, lanes):
    meta = jnp.concatenate([m[...] for m in metas], axis=0).astype(jnp.float32)
    total = meta.shape[0]
    ids = meta[:, :top]
    gains = meta[:, top : 2 * top] + meta[:, 2 * top : 3 * top] + meta[:, 3 * top : 4 * top]
    is_cold = ids == key_ref[0:1, :top]
    is_hot = ids == key_ref[1:2, :top]
    cold_gain = jnp.sum(jnp.where(is_cold, gains, 0.0), axis=1, keepdims=True)
    hot_gain = jnp.sum(jnp.where(is_hot, gains, 0.0), axis=1, keepdims=True)
    mark = jnp.sum(jnp.where(is_cold, 1.0, 0.0), axis=1, keepdims=True)
    marks = jnp.broadcast_to(mark, (total, lanes))
    shape = (total, total)
    below = lax.broadcasted_iota(jnp.int32, shape, 0) > lax.broadcasted_iota(jnp.int32, shape, 1)
    rank = mm(jnp.where(below, 1.0, 0.0).astype(jnp.bfloat16), marks.astype(jnp.bfloat16))
    lane = lax.broadcasted_iota(jnp.int32, (total, lanes), 1).astype(jnp.float32)
    spread = jnp.where((marks > 0.5) & (rank == lane), 1.0, 0.0).astype(jnp.bfloat16)
    return cold_gain, hot_gain, spread


def load_rows(blocks, x_ref):
    height, width = blocks[0].shape[0], x_ref.shape[1]
    for index, block in enumerate(blocks):
        x_ref[index * height : (index + 1) * height, :] = block[:, :width]


def tails(blocks, width):
    return [block.at[:, width : width + LANES] for block in blocks]


def weigh(hidden, packed_ref, spread, hot_ref, cold_gain, hot_gain, out_ref, first=0):
    width = out_ref.shape[1]
    rows = slice(first, first + hidden.shape[0])
    for start in range(0, width, STEP):
        at = slice(start, start + STEP)
        hot_part = mm(hidden, hot_ref[0, 2, :, at])
        cold_part = mm(spread, packed_ref[:, at])
        out_ref[rows, at] = (hot_gain * hot_part + cold_gain * cold_part).astype(out_ref.dtype)


def keep_gains(cold_gain, hot_gain, gain_ref):
    lane = lax.broadcasted_iota(jnp.int32, gain_ref.shape, 1)
    gain_ref[...] = jnp.where(lane == 0, cold_gain, hot_gain)


def early_kernel(n, top, cap, key_ref, *refs):
    blocks, (hot_ref, hid_ref, pick_ref, spread_ref, gain_ref, x_ref) = refs[:n], refs[n:]
    load_rows(blocks, x_ref)
    metas = tails(blocks, x_ref.shape[1])
    cold_gain, hot_gain, spread = routing(key_ref, metas, top, spread_ref.shape[1])
    spread_ref[...] = spread
    keep_gains(cold_gain, hot_gain, gain_ref)
    x = x_ref[...]
    hid_ref[...] = swish(mm(x, hot_ref[0, 0], NT), mm(x, hot_ref[0, 1], NT))
    pick_ref[...] = mm(spread[:, :cap], x, TN).astype(jnp.bfloat16)


def late_kernel(n, top, cap, key_ref, *refs):
    blocks, (early_ref, gate_up_ref, down_ref, hot_ref), rest = refs[:n], refs[n : n + 4], refs[n + 4 :]
    sib_ref, hid_ref, near_ref, far_ref, spread_ref, gain_ref, x_ref, c_ref, h_ref = rest
    width = x_ref.shape[1]
    units = down_ref.shape[1]
    load_rows(blocks, x_ref)
    cold_gain, hot_gain, spread = routing(key_ref, tails(blocks, width), top, spread_ref.shape[1])
    spread_ref[...] = spread
    keep_gains(cold_gain, hot_gain, gain_ref)
    spread = spread[:, :cap]
    x = x_ref[...]
    n_early = early_ref.shape[0]
    c_ref[:n_early, :] = early_ref[...]
    c_ref[n_early:, :] = mm(spread, x, TN).astype(jnp.bfloat16)
    cold = c_ref[...]
    for start in range(0, units, STEP):
        gate = mm(cold, gate_up_ref[0, :, start : start + STEP])
        up = mm(cold, gate_up_ref[0, :, units + start : units + start + STEP])
        h_ref[:, start : start + STEP] = swish(gate, up)
    hidden = swish(mm(x, hot_ref[0, 0], NT), mm(x, hot_ref[0, 1], NT))
    hid_ref[...] = hidden
    half = hidden.shape[0] // 2
    cold_hidden = h_ref[...]
    for start in range(0, width, STEP):
        at = slice(start, start + STEP)
        packed = mm(cold_hidden, down_ref[0, :, at]).astype(jnp.bfloat16)
        near_ref[:, at] = packed[:n_early]
        far_ref[:, at] = packed[n_early:]
    weigh(hidden[half:], far_ref, spread[half:], hot_ref, cold_gain[half:], hot_gain[half:], sib_ref)


def result_kernel(own_rows, sib_rows, after, hid_ref, packed_ref, spread_ref, gain_ref, hot_ref, *refs):
    outs = refs[after:]
    cap = packed_ref.shape[0]
    spans = ([sib_rows] if sib_rows else []) + [own_rows]
    for (first, size), out_ref in zip(spans, outs):
        at = slice(first, first + size)
        weigh(
            hid_ref[at, :],
            packed_ref,
            spread_ref[at, :cap],
            hot_ref,
            gain_ref[at, 0:1],
            gain_ref[at, 1:2],
            out_ref,
        )


def run_kernel(kernel, operands, outs, scratch, flops, moved, limit=12):
    vmem = pl.BlockSpec(memory_space=pltpu.VMEM)
    return pl.pallas_call(
        kernel,
        out_shape=[pltpu.VMEM(shape, dtype) for shape, dtype in outs],
        in_specs=[vmem] * len(operands),
        out_specs=[vmem] * len(outs),
        scratch_shapes=[pltpu.VMEM(shape, dtype) for shape, dtype in scratch],
        compiler_params=pltpu.CompilerParams(vmem_limit_bytes=limit * 2**20),
        cost_estimate=pl.CostEstimate(flops=flops, bytes_accessed=moved, transcendentals=0),
    )(*[pin(a) for a in operands])


def load_weights(weights, after):
    n = len(weights)
    hbm = lambda a: pltpu.with_memory_space_constraint(a, pltpu.HBM)
    return pl.pallas_call(
        functools.partial(load_kernel, n),
        out_shape=[pltpu.VMEM(w.shape, w.dtype) for w in weights],
        in_specs=[pl.BlockSpec(memory_space=pltpu.HBM)] * n + [pl.BlockSpec(memory_space=pl.ANY)],
        out_specs=[pl.BlockSpec(memory_space=pltpu.VMEM)] * n,
        scratch_shapes=[pltpu.SemaphoreType.DMA((4 * n + 8,))],
        compiler_params=pltpu.CompilerParams(vmem_limit_bytes=2**20),
        cost_estimate=pl.CostEstimate(
            flops=0, bytes_accessed=sum(w.size * 2 for w in weights), transcendentals=0
        ),
    )(*[hbm(w) for w in weights], after)


def make_message(tokens, ids, gains, hot_list, slot_of):
    rows, width = tokens.shape
    vmem, smem = pl.BlockSpec(memory_space=pltpu.VMEM), pl.BlockSpec(memory_space=pltpu.SMEM)
    hbm = lambda a: pltpu.with_memory_space_constraint(a, pltpu.HBM)
    return pl.pallas_call(
        message_kernel,
        out_shape=[
            pltpu.VMEM((rows, width + LANES), tokens.dtype),
            pltpu.VMEM((8, LANES), jnp.float32),
        ],
        in_specs=[smem] * 2 + [vmem] * 3,
        out_specs=[vmem] * 2,
        compiler_params=pltpu.CompilerParams(vmem_limit_bytes=2**21),
    )(*[hbm(a) for a in (hot_list, slot_of, tokens, ids, gains)])


def ring_perms(n_dp):
    chips = [(0, z) for z in range(n_dp)] + [(1, z) for z in reversed(range(n_dp))]
    size = len(chips)

    def device(place, core):
        x, z = chips[place % size]
        return (2 * x + core) * n_dp + z

    def hop(by):
        return [
            (device(i, core), device(i + (-by if core else by), core))
            for i in range(size)
            for core in range(2)
        ]

    swap = [(device(i, core), device(i, 1 - core)) for i in range(size) for core in range(2)]
    return hop, swap


def dense_body(tokens, expert_ids, route_w, hot_list, slot_of, cold_gate_up, cold_down, hot_weights):
    tok_rows, width = tokens.shape
    top = expert_ids.shape[1]
    n_hot, n_exp = hot_list.shape[0], slot_of.shape[0]
    n_dp = lax.axis_size("dp")
    units, hot_units = cold_down.shape[1], hot_weights.shape[3]
    cold_cap = -(-(tok_rows * top - n_hot * tok_rows) // (n_exp - n_hot))
    f32, bf16 = jnp.float32, jnp.bfloat16
    hop, swap_pairs = ring_perms(n_dp)
    axes = ("ep", "dp")
    move = lambda a, by: lax.ppermute(a, axes, hop(by))
    swap = lambda a: lax.ppermute(a, axes, swap_pairs)

    message, key = make_message(tokens, expert_ids.T, route_w.T, hot_list, slot_of)
    weights = (cold_gate_up, cold_down, jnp.swapaxes(hot_weights, 2, 3))
    gate_up, down, hot = load_weights(weights, message)

    tie = lambda *arrays: lax.optimization_barrier(arrays)
    own = {0: message}
    own[1], own[-1], hot = tie(move(message, 1), move(message, -1), hot)
    own[2], own[-2] = tie(move(own[1], 1), move(own[-1], -1))
    own[4], own[3], own[-3] = move(own[2], 2), move(own[2], 1), move(own[-2], -1)
    sib = {far: swap(own[far]) for far in own}

    near, late = (2, -2, 1, -1, 0), (4, 3, -3)
    pad = lambda n: -(-n * cold_cap // 16) * 16
    lanes = lambda cap: -(-cap // LANES) * LANES
    n_near, n_late = 2 * len(near), 2 * len(late)
    cap_near, cap_late = pad(n_near), pad(n_late)
    rows_near, rows_late = n_near * tok_rows, n_late * tok_rows
    gather = lambda fars: [own[f] for f in fars] + [sib[f] for f in fars]
    hid_near, picked, spread_near, gain_near = run_kernel(
        functools.partial(early_kernel, n_near, top, cap_near),
        (key, *gather(near), hot),
        [
            ((rows_near, hot_units), bf16),
            ((cap_near, width), bf16),
            ((rows_near, lanes(cap_near)), bf16),
            ((rows_near, LANES), f32),
        ],
        [((rows_near, width), bf16)],
        2 * rows_near * width * (2 * hot_units + cap_near),
        4 * rows_near * width,
    )
    back_late, hid_late, packed_near, packed_late, spread_late, gain_late = run_kernel(
        functools.partial(late_kernel, n_late, top, cap_late),
        (key, *gather(late), picked, gate_up, down, hot),
        [
            ((rows_late // 2, width), bf16),
            ((rows_late, hot_units), bf16),
            ((cap_near, width), bf16),
            ((cap_late, width), bf16),
            ((rows_late, lanes(cap_late)), bf16),
            ((rows_late, LANES), f32),
        ],
        [
            ((rows_late, width), bf16),
            ((cap_near + cap_late, width), bf16),
            ((cap_near + cap_late, units), bf16),
        ],
        2 * (cap_near + cap_late) * 3 * units * width,
        4 * rows_late * width,
    )

    def results(fars, pool, sides, after=()):
        hid, packed, spread, gain = sides
        first, size = pool.index(fars[0]) * tok_rows, len(fars) * tok_rows
        shift = len(pool) * tok_rows
        outs = [((size, width), f32)]
        if pool is near:
            outs = [((size, width), bf16)] + outs
        return run_kernel(
            functools.partial(
                result_kernel,
                (first, size),
                (first + shift, size) if pool is near else None,
                len(after),
            ),
            (hid, packed, spread, gain, hot, *after),
            outs,
            [],
            4 * size * width * (hot_units + packed.shape[0]),
            8 * size * width,
        )

    total = {}

    def add_up(fars, mine, other):
        for index, far in enumerate(fars):
            at = slice(index * tok_rows, (index + 1) * tok_rows)
            total[far] = mine[at] + other[at].astype(f32)

    low = lambda a: a.astype(bf16)
    sides = (hid_near, packed_near, spread_near, gain_near)
    from_late = swap(back_late)
    (own_late,) = results(late, late, (hid_late, packed_late, spread_late, gain_late))
    add_up(late, own_late, from_late)
    first, ahead, behind = tie(low(total[4]), low(total[-3]), low(total[3]))
    back, mine = results(near, near, sides, (first,))
    first, ahead, behind = move(first, -2), move(ahead, 1), move(behind, -1)
    add_up(near, mine, swap(back))
    total[2] = total[2] + first.astype(f32)
    for far in (2, 1):
        ahead, behind = tie(ahead, behind)
        ahead, behind = tie(low(total[-far] + ahead.astype(f32)), low(total[far] + behind.astype(f32)))
        ahead, behind = move(ahead, 1), move(behind, -1)
    return low(total[0] + ahead.astype(f32) + behind.astype(f32))


def body(tokens, expert_ids, *rest):
    hot_list, slot_of = rest[1], rest[2]
    every_row_hot = 2 * expert_ids.shape[1] == slot_of.shape[0]
    two_columns = lax.axis_size("ep") == 4 and lax.axis_size("dp") == 4
    chosen = dense_body if every_row_hot and two_columns else routed_body
    return chosen(tokens, expert_ids, *rest)


def solution(mesh):
    in_specs = (
        P(("groups", "ep", "dp"), None),
        P(("groups", "ep", "dp"), None),
        P(("groups", "ep", "dp"), None),
        P("groups"),
        P(),
        P(("ep", "dp"), None, None),
        P(("ep", "dp"), None, None),
        P("dp", None, None, "ep"),
    )
    out_specs = P(("groups", "ep", "dp"), None)
    return jax.shard_map(body, mesh=mesh, in_specs=in_specs, out_specs=out_specs, check_vma=False)
```

```python
import functools

import jax
import jax.numpy as jnp
from jax import lax
from jax.experimental import pallas as pl
from jax.experimental.pallas import tpu as pltpu
from jax.sharding import PartitionSpec as P


def swiglu_rows(inputs, gate_up, down_proj):
    in_shape = inputs.shape
    flat_in = inputs.reshape(-1, in_shape[-1])
    hidden_width = down_proj.shape[0]
    both_out = jnp.dot(flat_in, gate_up, preferred_element_type=jnp.float32)
    hidden = (jax.nn.silu(both_out[:, :hidden_width]) * both_out[:, hidden_width:]).astype(
        jnp.bfloat16
    )
    result = jnp.dot(hidden, down_proj, preferred_element_type=jnp.float32)
    return result.astype(jnp.bfloat16).reshape(in_shape)


def sliced_rows(inputs, triple):
    in_shape = inputs.shape
    flat_in = inputs.reshape(-1, in_shape[-1])
    gate_out = jnp.dot(flat_in, triple[0], preferred_element_type=jnp.float32)
    up_out = jnp.dot(flat_in, triple[1], preferred_element_type=jnp.float32)
    hidden = (jax.nn.silu(gate_out) * up_out).astype(jnp.bfloat16)
    result = lax.dot_general(
        hidden, triple[2], (((1,), (1,)), ((), ())), preferred_element_type=jnp.float32
    )
    return result.reshape(in_shape)


def routed_body(tokens, expert_ids, route_w, hot_list, slot_of, cold_gate_up, cold_down, hot_weights):
    tok_rows, model_width = tokens.shape
    top_count = expert_ids.shape[1]
    n_hot = hot_list.shape[0]
    n_exp = slot_of.shape[0]
    n_ep = lax.axis_size("ep")
    n_dp = lax.axis_size("dp")
    n_dev = n_ep * n_dp
    most_rows = 2 * tok_rows * top_count // n_exp
    spare_rows = tok_rows * top_count - n_hot * most_rows
    cold_cap = (spare_rows + n_exp - n_hot - 1) // (n_exp - n_hot)
    one_hot = expert_ids[:, :, None] == jnp.arange(n_exp, dtype=jnp.int32)[None, None, :]
    slot_ids = jnp.sum(jnp.where(one_hot, slot_of[None, None, :], 0), axis=2)
    hot_match = expert_ids[:, :, None] == hot_list[None, None, :]
    is_hot = jnp.any(hot_match, axis=2)
    hot_index = jnp.sum(
        jnp.where(hot_match, jnp.arange(n_hot, dtype=jnp.int32)[None, None, :], 0), axis=2
    )
    flat_onehot = one_hot.reshape(tok_rows * top_count, n_exp).astype(jnp.int32)
    earlier = jnp.cumsum(flat_onehot, axis=0) - flat_onehot
    rank_ids = jnp.sum(earlier * flat_onehot, axis=1).reshape(tok_rows, top_count)
    row_ids = jnp.broadcast_to(
        jnp.arange(tok_rows, dtype=jnp.int32)[:, None], (tok_rows, top_count)
    ).reshape(-1)
    cold_size = n_dev * cold_cap
    hot_size = n_hot * most_rows
    cold_target = jnp.where(is_hot, cold_size, slot_ids * cold_cap + rank_ids).reshape(-1)
    hot_target = jnp.where(is_hot, hot_index * most_rows + rank_ids, hot_size).reshape(-1)
    cold_map = jnp.full((cold_size,), tok_rows, jnp.int32).at[cold_target].set(row_ids, mode="drop")
    hot_map = jnp.full((hot_size,), tok_rows, jnp.int32).at[hot_target].set(row_ids, mode="drop")
    padded = jnp.concatenate([tokens, jnp.zeros((1, model_width), tokens.dtype)], axis=0)
    cold_send = jnp.take(padded, cold_map, axis=0).reshape(n_dev, cold_cap, model_width)
    hot_send = jnp.take(padded, hot_map, axis=0).reshape(n_hot, most_rows, model_width)
    gate_up = cold_gate_up[0]
    down_proj = cold_down[0]
    cold_back = lax.all_to_all(
        swiglu_rows(
            lax.all_to_all(cold_send, ("ep", "dp"), split_axis=0, concat_axis=0, tiled=True),
            gate_up,
            down_proj,
        ),
        ("ep", "dp"),
        split_axis=0,
        concat_axis=0,
        tiled=True,
    )
    hot_recv = lax.all_to_all(hot_send, "dp", split_axis=0, concat_axis=0, tiled=True)
    gathered = lax.all_gather(hot_recv, "ep", axis=0, tiled=True)
    own_slice = hot_weights[0]
    hot_sum = lax.psum_scatter(
        sliced_rows(gathered, own_slice), "ep", scatter_dimension=0, tiled=True
    )
    hot_back = lax.all_to_all(
        hot_sum.astype(jnp.bfloat16), "dp", split_axis=0, concat_axis=0, tiled=True
    )
    answers = jnp.concatenate(
        [cold_back.reshape(cold_size, model_width), hot_back.reshape(hot_size, model_width)], axis=0
    )
    positions = jnp.where(
        is_hot, cold_size + hot_index * most_rows + rank_ids, slot_ids * cold_cap + rank_ids
    )
    picked = jnp.take(answers, positions, axis=0)
    mixed = jnp.zeros((tok_rows, model_width), jnp.float32)
    for column in range(top_count):
        mixed = mixed + route_w[:, column, None] * picked[:, column].astype(jnp.float32)
    return mixed.astype(jnp.bfloat16)


def pin(array):
    return pltpu.with_memory_space_constraint(array, pltpu.VMEM)


NN = (((1,), (0,)), ((), ()))
NT = (((1,), (1,)), ((), ()))
TN = (((0,), (0,)), ((), ()))
STEP = 256
LANES = 128


def mm(a, b, dims=NN):
    return lax.dot_general(a, b, dims, preferred_element_type=jnp.float32)


def swish(gate, up):
    return (gate / (1.0 + jnp.exp(-gate)) * up).astype(jnp.bfloat16)


def message_kernel(hot_list_ref, slot_ref, *refs):
    out_ref, key_ref = refs[-2:]
    bf16, f32 = jnp.bfloat16, jnp.float32
    for half in range(2):
        tok_ref, ids_ref, gain_ref = refs[3 * half : 3 * half + 3]
        height, width = tok_ref.shape
        at = slice(half * height, (half + 1) * height)
        out_ref[at, :width] = tok_ref[...]
        gains = gain_ref[...]
        terms = [ids_ref[...].astype(f32)]
        for _ in range(3):
            term = gains.astype(bf16).astype(f32)
            terms.append(term)
            gains = gains - term
        stacked = jnp.concatenate(terms, axis=0).astype(bf16)
        shape = (stacked.shape[0], LANES)
        row, lane = (lax.broadcasted_iota(jnp.int32, shape, axis) for axis in (0, 1))
        place = jnp.where(row == lane, 1.0, 0.0).astype(bf16)
        out_ref[at, width:] = mm(stacked, place, TN).astype(bf16)
    along = lax.axis_index("dp")
    me = lax.axis_index("ep") * lax.axis_size("dp") + along
    my_cold, my_hot = jnp.int32(0), jnp.int32(0)
    for expert in range(slot_ref.shape[0]):
        my_cold = jnp.where(slot_ref[expert] == me, expert, my_cold)
    held = my_cold
    for place in range(hot_list_ref.shape[0]):
        my_cold = jnp.where(hot_list_ref[place] == held, -1, my_cold)
        my_hot = jnp.where(along == place, hot_list_ref[place], my_hot)
    row = lax.broadcasted_iota(jnp.int32, key_ref.shape, 0)
    key_ref[...] = jnp.where(row == 0, my_cold, my_hot).astype(f32)


def load_kernel(n, *refs):
    copies = []
    sems = refs[2 * n + 1]
    for index in range(n):
        src, dst = refs[index], refs[n + 1 + index]
        rows = src.shape[-2]
        parts = 4
        for part in range(parts):
            at = pl.ds(part * (rows // parts), rows // parts)
            lead = (0,) * (len(src.shape) - 2)
            if len(src.shape) == 4:
                for third in range(src.shape[1]):
                    copies.append((src.at[0, third, at], dst.at[0, third, at]))
            else:
                copies.append((src.at[lead + (at,)], dst.at[lead + (at,)]))
    started = []
    for number, (src, dst) in enumerate(copies):
        copy = pltpu.make_async_copy(src, dst, sems.at[number])
        copy.start()
        started.append(copy)
    for copy in started:
        copy.wait()


def routing(key_ref, meta, top, lanes):
    meta = meta.astype(jnp.float32)
    total = meta.shape[0]
    ids = meta[:, :top]
    gains = meta[:, top : 2 * top] + meta[:, 2 * top : 3 * top] + meta[:, 3 * top : 4 * top]
    is_cold = ids == key_ref[0:1, :top]
    is_hot = ids == key_ref[1:2, :top]
    cold_gain = jnp.sum(jnp.where(is_cold, gains, 0.0), axis=1, keepdims=True)
    hot_gain = jnp.sum(jnp.where(is_hot, gains, 0.0), axis=1, keepdims=True)
    mark = jnp.sum(jnp.where(is_cold, 1.0, 0.0), axis=1, keepdims=True)
    marks = jnp.broadcast_to(mark, (total, lanes))
    shape = (total, total)
    below = lax.broadcasted_iota(jnp.int32, shape, 0) > lax.broadcasted_iota(jnp.int32, shape, 1)
    rank = mm(jnp.where(below, 1.0, 0.0).astype(jnp.bfloat16), marks.astype(jnp.bfloat16))
    lane = lax.broadcasted_iota(jnp.int32, (total, lanes), 1).astype(jnp.float32)
    spread = jnp.where((marks > 0.5) & (rank == lane), 1.0, 0.0).astype(jnp.bfloat16)
    return cold_gain, hot_gain, spread


def load_rows(blocks, spans, x_ref):
    width, at, tails = x_ref.shape[1], 0, []
    for block, (first, size) in zip(blocks, spans):
        x_ref[at : at + size, :] = block[first : first + size, :width]
        tails.append(block[first : first + size, width : width + LANES])
        at += size
    return jnp.concatenate(tails, axis=0)


def weigh(hidden, packed_ref, spread, hot_ref, cold_gain, hot_gain, out_ref, first=0):
    width = out_ref.shape[1]
    rows = slice(first, first + hidden.shape[0])
    for start in range(0, width, STEP):
        at = slice(start, start + STEP)
        hot_part = mm(hidden, hot_ref[0, 2, :, at])
        cold_part = mm(spread, packed_ref[:, at])
        out_ref[rows, at] = (hot_gain * hot_part + cold_gain * cold_part).astype(out_ref.dtype)


def keep_gains(cold_gain, hot_gain, gain_ref):
    lane = lax.broadcasted_iota(jnp.int32, gain_ref.shape, 1)
    gain_ref[...] = jnp.where(lane == 0, cold_gain, hot_gain)


def early_kernel(spans, top, cap, key_ref, *refs):
    n = len(spans)
    hot_ref, hid_ref, pick_ref, spread_ref, gain_ref, x_ref = refs[n:]
    meta = load_rows(refs[:n], spans, x_ref)
    cold_gain, hot_gain, spread = routing(key_ref, meta, top, spread_ref.shape[1])
    spread_ref[...] = spread
    keep_gains(cold_gain, hot_gain, gain_ref)
    x = x_ref[...]
    hid_ref[...] = swish(mm(x, hot_ref[0, 0], NT), mm(x, hot_ref[0, 1], NT))
    pick_ref[...] = mm(spread[:, :cap], x, TN).astype(jnp.bfloat16)


def late_kernel(spans, top, cap, key_ref, *refs):
    n = len(spans)
    (early_ref, gate_up_ref, down_ref, hot_ref), rest = refs[n : n + 4], refs[n + 4 :]
    sib_ref, hid_ref, near_ref, far_ref, spread_ref, gain_ref, x_ref, c_ref, h_ref = rest
    width = x_ref.shape[1]
    units = down_ref.shape[1]
    meta = load_rows(refs[:n], spans, x_ref)
    cold_gain, hot_gain, spread = routing(key_ref, meta, top, spread_ref.shape[1])
    spread_ref[...] = spread
    keep_gains(cold_gain, hot_gain, gain_ref)
    spread = spread[:, :cap]
    x = x_ref[...]
    n_early = early_ref.shape[0]
    c_ref[:n_early, :] = early_ref[...]
    c_ref[n_early:, :] = mm(spread, x, TN).astype(jnp.bfloat16)
    cold = c_ref[...]
    for start in range(0, units, STEP):
        gate = mm(cold, gate_up_ref[0, :, start : start + STEP])
        up = mm(cold, gate_up_ref[0, :, units + start : units + start + STEP])
        h_ref[:, start : start + STEP] = swish(gate, up)
    hidden = swish(mm(x, hot_ref[0, 0], NT), mm(x, hot_ref[0, 1], NT))
    hid_ref[...] = hidden
    half = hidden.shape[0] // 2
    cold_hidden = h_ref[...]
    for start in range(0, width, STEP):
        at = slice(start, start + STEP)
        packed = mm(cold_hidden, down_ref[0, :, at]).astype(jnp.bfloat16)
        near_ref[:, at] = packed[:n_early]
        far_ref[:, at] = packed[n_early:]
    weigh(hidden[half:], far_ref, spread[half:], hot_ref, cold_gain[half:], hot_gain[half:], sib_ref)


def result_kernel(own_rows, sib_rows, after, hid_ref, packed_ref, spread_ref, gain_ref, hot_ref, *refs):
    outs = refs[after:]
    cap = packed_ref.shape[0]
    spans = ([sib_rows] if sib_rows else []) + [own_rows]
    for (first, size), out_ref in zip(spans, outs):
        at = slice(first, first + size)
        weigh(
            hid_ref[at, :],
            packed_ref,
            spread_ref[at, :cap],
            hot_ref,
            gain_ref[at, 0:1],
            gain_ref[at, 1:2],
            out_ref,
        )


def run_kernel(kernel, operands, outs, scratch, flops, moved, limit=12):
    vmem = pl.BlockSpec(memory_space=pltpu.VMEM)
    return pl.pallas_call(
        kernel,
        out_shape=[pltpu.VMEM(shape, dtype) for shape, dtype in outs],
        in_specs=[vmem] * len(operands),
        out_specs=[vmem] * len(outs),
        scratch_shapes=[pltpu.VMEM(shape, dtype) for shape, dtype in scratch],
        compiler_params=pltpu.CompilerParams(vmem_limit_bytes=limit * 2**20),
        cost_estimate=pl.CostEstimate(flops=flops, bytes_accessed=moved, transcendentals=0),
    )(*[pin(a) for a in operands])


def load_weights(weights, after):
    n = len(weights)
    hbm = lambda a: pltpu.with_memory_space_constraint(a, pltpu.HBM)
    return pl.pallas_call(
        functools.partial(load_kernel, n),
        out_shape=[pltpu.VMEM(w.shape, w.dtype) for w in weights],
        in_specs=[pl.BlockSpec(memory_space=pltpu.HBM)] * n + [pl.BlockSpec(memory_space=pl.ANY)],
        out_specs=[pl.BlockSpec(memory_space=pltpu.VMEM)] * n,
        scratch_shapes=[pltpu.SemaphoreType.DMA((4 * n + 8,))],
        compiler_params=pltpu.CompilerParams(vmem_limit_bytes=2**20),
        cost_estimate=pl.CostEstimate(
            flops=0, bytes_accessed=sum(w.size * 2 for w in weights), transcendentals=0
        ),
    )(*[hbm(w) for w in weights], after)


def make_message(hot_list, slot_of, *sides):
    rows, width = sides[0].shape
    vmem, smem = pl.BlockSpec(memory_space=pltpu.VMEM), pl.BlockSpec(memory_space=pltpu.SMEM)
    hbm = lambda a: pltpu.with_memory_space_constraint(a, pltpu.HBM)
    return pl.pallas_call(
        message_kernel,
        out_shape=[
            pltpu.VMEM((2 * rows, width + LANES), sides[0].dtype),
            pltpu.VMEM((8, LANES), jnp.float32),
        ],
        in_specs=[smem] * 2 + [vmem] * 6,
        out_specs=[vmem] * 2,
        compiler_params=pltpu.CompilerParams(vmem_limit_bytes=2**21),
    )(hbm(hot_list), hbm(slot_of), *[hbm(a) for a in sides[:3]], *[pin(a) for a in sides[3:]])


def ring_perms(n_dp):
    chips = [(0, z) for z in range(n_dp)] + [(1, z) for z in reversed(range(n_dp))]
    size = len(chips)

    def device(place, core):
        x, z = chips[place % size]
        return (2 * x + core) * n_dp + z

    def hop(by, cross):
        return [
            (device(i, core), device(i + (-by if core else by), core ^ cross))
            for i in range(size)
            for core in range(2)
        ]

    swap = [(device(i, core), device(i, 1 - core)) for i in range(size) for core in range(2)]
    return hop, swap


def dense_body(tokens, expert_ids, route_w, hot_list, slot_of, cold_gate_up, cold_down, hot_weights):
    tok_rows, width = tokens.shape
    top = expert_ids.shape[1]
    n_hot, n_exp = hot_list.shape[0], slot_of.shape[0]
    n_dp = lax.axis_size("dp")
    units, hot_units = cold_down.shape[1], hot_weights.shape[3]
    cold_cap = -(-(tok_rows * top - n_hot * tok_rows) // (n_exp - n_hot))
    f32, bf16 = jnp.float32, jnp.bfloat16
    hop, swap_pairs = ring_perms(n_dp)
    axes = ("ep", "dp")
    move = lambda a, by: lax.ppermute(a, axes, hop(by, 0))
    cross = lambda a, by: lax.ppermute(a, axes, hop(by, 1))
    swap = lambda a: lax.ppermute(a, axes, swap_pairs)
    tie = lambda *arrays: lax.optimization_barrier(arrays)

    given = (tokens, expert_ids, route_w)
    sides = [a for side in (given, [swap(a) for a in given]) for a in side]
    sides = [a.T if index % 3 else a for index, a in enumerate(sides)]
    message, key = make_message(hot_list, slot_of, *sides)
    weights = (cold_gate_up, cold_down, jnp.swapaxes(hot_weights, 2, 3))
    gate_up, down, hot = load_weights(weights, message)

    two = move(message, 2)
    later, hot = tie(message, hot)
    one = move(later, 1)
    two, hot = tie(two, hot)
    four, three = move(two[:tok_rows], 2), move(two, 1)

    whole, half, rest = (0, 2 * tok_rows), (0, tok_rows), (tok_rows, tok_rows)
    near_rows = ((two, whole), (one, whole), (message, half), (swap(two), whole), (swap(one), whole), (message, rest))
    late_rows = ((four, half), (three, whole), (swap(four), half), (swap(three), whole))
    pad = lambda n: -(-n * cold_cap // 16) * 16
    lanes = lambda cap: -(-cap // LANES) * LANES
    rows_near, rows_late = (sum(span[1] for _, span in rows) for rows in (near_rows, late_rows))
    cap_near, cap_late = pad(rows_near // tok_rows), pad(rows_late // tok_rows)
    hid_near, picked, spread_near, gain_near = run_kernel(
        functools.partial(early_kernel, [span for _, span in near_rows], top, cap_near),
        (key, *[a for a, _ in near_rows], hot),
        [
            ((rows_near, hot_units), bf16),
            ((cap_near, width), bf16),
            ((rows_near, lanes(cap_near)), bf16),
            ((rows_near, LANES), f32),
        ],
        [((rows_near, width), bf16)],
        2 * rows_near * width * (2 * hot_units + cap_near),
        4 * rows_near * width,
    )
    back_late, hid_late, packed_near, packed_late, spread_late, gain_late = run_kernel(
        functools.partial(late_kernel, [span for _, span in late_rows], top, cap_late),
        (key, *[a for a, _ in late_rows], picked, gate_up, down, hot),
        [
            ((rows_late // 2, width), bf16),
            ((rows_late, hot_units), bf16),
            ((cap_near, width), bf16),
            ((cap_late, width), bf16),
            ((rows_late, lanes(cap_late)), bf16),
            ((rows_late, LANES), f32),
        ],
        [
            ((rows_late, width), bf16),
            ((cap_near + cap_late, width), bf16),
            ((cap_near + cap_late, units), bf16),
        ],
        2 * (cap_near + cap_late) * 3 * units * width,
        4 * rows_late * width,
    )

    def results(size, both, hid, packed, spread, gain):
        outs = [((size, width), bf16)] if both else []
        return run_kernel(
            functools.partial(result_kernel, (0, size), (size, size) if both else None, 0),
            (hid, packed, spread, gain, hot),
            outs + [((size, width), f32)],
            [],
            4 * size * width * (hot_units + packed.shape[0]),
            8 * size * width,
        )

    low = lambda a: a.astype(bf16)
    from_late = swap(back_late)
    (mine_late,) = results(rows_late // 2, False, hid_late, packed_late, spread_late, gain_late)
    back, mine = results(rows_near // 2, True, hid_near, packed_near, spread_near, gain_near)
    from_late, mine = tie(from_late, mine)
    late = mine_late + from_late.astype(f32)
    fourth, third = tie(low(late[:tok_rows]), low(late[tok_rows:]))
    fourth, third = move(fourth, -2).astype(f32), move(third, -1).astype(f32)
    near = mine + swap(back).astype(f32)
    part = lambda index: near[index * tok_rows : (index + 1) * tok_rows]
    far = tie(low(part(0) + third[:tok_rows] + fourth), low(part(1) + third[tok_rows:]))
    close = move(low(near[2 * tok_rows : 4 * tok_rows]), -1)
    parts = (close[:tok_rows], swap(close[tok_rows:]), move(far[0], -2), cross(far[1], -2))
    return low(sum((a.astype(f32) for a in parts), part(4)))


def body(tokens, expert_ids, *rest):
    hot_list, slot_of = rest[1], rest[2]
    every_row_hot = 2 * expert_ids.shape[1] == slot_of.shape[0]
    two_columns = lax.axis_size("ep") == 4 and lax.axis_size("dp") == 4
    chosen = dense_body if every_row_hot and two_columns else routed_body
    return chosen(tokens, expert_ids, *rest)


def solution(mesh):
    in_specs = (
        P(("groups", "ep", "dp"), None),
        P(("groups", "ep", "dp"), None),
        P(("groups", "ep", "dp"), None),
        P("groups"),
        P(),
        P(("ep", "dp"), None, None),
        P(("ep", "dp"), None, None),
        P("dp", None, None, "ep"),
    )
    out_specs = P(("groups", "ep", "dp"), None)
    return jax.shard_map(body, mesh=mesh, in_specs=in_specs, out_specs=out_specs, check_vma=False)
```

```python
import functools

import jax
import jax.numpy as jnp
from jax import lax
from jax.experimental import pallas as pl
from jax.experimental.pallas import tpu as pltpu
from jax.sharding import PartitionSpec as P


def swiglu_rows(inputs, gate_up, down_proj):
    in_shape = inputs.shape
    flat_in = inputs.reshape(-1, in_shape[-1])
    hidden_width = down_proj.shape[0]
    both_out = jnp.dot(flat_in, gate_up, preferred_element_type=jnp.float32)
    hidden = (jax.nn.silu(both_out[:, :hidden_width]) * both_out[:, hidden_width:]).astype(
        jnp.bfloat16
    )
    result = jnp.dot(hidden, down_proj, preferred_element_type=jnp.float32)
    return result.astype(jnp.bfloat16).reshape(in_shape)


def sliced_rows(inputs, triple):
    in_shape = inputs.shape
    flat_in = inputs.reshape(-1, in_shape[-1])
    gate_out = jnp.dot(flat_in, triple[0], preferred_element_type=jnp.float32)
    up_out = jnp.dot(flat_in, triple[1], preferred_element_type=jnp.float32)
    hidden = (jax.nn.silu(gate_out) * up_out).astype(jnp.bfloat16)
    result = lax.dot_general(
        hidden, triple[2], (((1,), (1,)), ((), ())), preferred_element_type=jnp.float32
    )
    return result.reshape(in_shape)


def routed_body(tokens, expert_ids, route_w, hot_list, slot_of, cold_gate_up, cold_down, hot_weights):
    tok_rows, model_width = tokens.shape
    top_count = expert_ids.shape[1]
    n_hot = hot_list.shape[0]
    n_exp = slot_of.shape[0]
    n_ep = lax.axis_size("ep")
    n_dp = lax.axis_size("dp")
    n_dev = n_ep * n_dp
    most_rows = 2 * tok_rows * top_count // n_exp
    spare_rows = tok_rows * top_count - n_hot * most_rows
    cold_cap = (spare_rows + n_exp - n_hot - 1) // (n_exp - n_hot)
    one_hot = expert_ids[:, :, None] == jnp.arange(n_exp, dtype=jnp.int32)[None, None, :]
    slot_ids = jnp.sum(jnp.where(one_hot, slot_of[None, None, :], 0), axis=2)
    hot_match = expert_ids[:, :, None] == hot_list[None, None, :]
    is_hot = jnp.any(hot_match, axis=2)
    hot_index = jnp.sum(
        jnp.where(hot_match, jnp.arange(n_hot, dtype=jnp.int32)[None, None, :], 0), axis=2
    )
    flat_onehot = one_hot.reshape(tok_rows * top_count, n_exp).astype(jnp.int32)
    earlier = jnp.cumsum(flat_onehot, axis=0) - flat_onehot
    rank_ids = jnp.sum(earlier * flat_onehot, axis=1).reshape(tok_rows, top_count)
    row_ids = jnp.broadcast_to(
        jnp.arange(tok_rows, dtype=jnp.int32)[:, None], (tok_rows, top_count)
    ).reshape(-1)
    cold_size = n_dev * cold_cap
    hot_size = n_hot * most_rows
    cold_target = jnp.where(is_hot, cold_size, slot_ids * cold_cap + rank_ids).reshape(-1)
    hot_target = jnp.where(is_hot, hot_index * most_rows + rank_ids, hot_size).reshape(-1)
    cold_map = jnp.full((cold_size,), tok_rows, jnp.int32).at[cold_target].set(row_ids, mode="drop")
    hot_map = jnp.full((hot_size,), tok_rows, jnp.int32).at[hot_target].set(row_ids, mode="drop")
    padded = jnp.concatenate([tokens, jnp.zeros((1, model_width), tokens.dtype)], axis=0)
    cold_send = jnp.take(padded, cold_map, axis=0).reshape(n_dev, cold_cap, model_width)
    hot_send = jnp.take(padded, hot_map, axis=0).reshape(n_hot, most_rows, model_width)
    gate_up = cold_gate_up[0]
    down_proj = cold_down[0]
    cold_back = lax.all_to_all(
        swiglu_rows(
            lax.all_to_all(cold_send, ("ep", "dp"), split_axis=0, concat_axis=0, tiled=True),
            gate_up,
            down_proj,
        ),
        ("ep", "dp"),
        split_axis=0,
        concat_axis=0,
        tiled=True,
    )
    hot_recv = lax.all_to_all(hot_send, "dp", split_axis=0, concat_axis=0, tiled=True)
    gathered = lax.all_gather(hot_recv, "ep", axis=0, tiled=True)
    own_slice = hot_weights[0]
    hot_sum = lax.psum_scatter(
        sliced_rows(gathered, own_slice), "ep", scatter_dimension=0, tiled=True
    )
    hot_back = lax.all_to_all(
        hot_sum.astype(jnp.bfloat16), "dp", split_axis=0, concat_axis=0, tiled=True
    )
    answers = jnp.concatenate(
        [cold_back.reshape(cold_size, model_width), hot_back.reshape(hot_size, model_width)], axis=0
    )
    positions = jnp.where(
        is_hot, cold_size + hot_index * most_rows + rank_ids, slot_ids * cold_cap + rank_ids
    )
    picked = jnp.take(answers, positions, axis=0)
    mixed = jnp.zeros((tok_rows, model_width), jnp.float32)
    for column in range(top_count):
        mixed = mixed + route_w[:, column, None] * picked[:, column].astype(jnp.float32)
    return mixed.astype(jnp.bfloat16)


def pin(array):
    return pltpu.with_memory_space_constraint(array, pltpu.VMEM)


NN = (((1,), (0,)), ((), ()))
NT = (((1,), (1,)), ((), ()))
TN = (((0,), (0,)), ((), ()))
STEP = 256
LANES = 128


def mm(a, b, dims=NN):
    return lax.dot_general(a, b, dims, preferred_element_type=jnp.float32)


def swish(gate, up):
    return (gate / (1.0 + jnp.exp(-gate)) * up).astype(jnp.bfloat16)


def message_kernel(hot_list_ref, slot_ref, tok_ref, ids_ref, gain_ref, out_ref, key_ref):
    width = tok_ref.shape[1]
    out_ref[:, :width] = tok_ref[...]
    bf16, f32 = jnp.bfloat16, jnp.float32
    gains = gain_ref[...]
    terms = [ids_ref[...].astype(f32)]
    for _ in range(3):
        term = gains.astype(bf16).astype(f32)
        terms.append(term)
        gains = gains - term
    stacked = jnp.concatenate(terms, axis=0).astype(bf16)
    shape = (stacked.shape[0], LANES)
    row, lane = (lax.broadcasted_iota(jnp.int32, shape, axis) for axis in (0, 1))
    place = jnp.where(row == lane, 1.0, 0.0).astype(bf16)
    out_ref[:, width:] = mm(stacked, place, TN).astype(bf16)
    along = lax.axis_index("dp")
    me = lax.axis_index("ep") * lax.axis_size("dp") + along
    my_cold, my_hot = jnp.int32(0), jnp.int32(0)
    for expert in range(slot_ref.shape[0]):
        my_cold = jnp.where(slot_ref[expert] == me, expert, my_cold)
    held = my_cold
    for place in range(hot_list_ref.shape[0]):
        my_cold = jnp.where(hot_list_ref[place] == held, -1, my_cold)
        my_hot = jnp.where(along == place, hot_list_ref[place], my_hot)
    row = lax.broadcasted_iota(jnp.int32, key_ref.shape, 0)
    key_ref[...] = jnp.where(row == 0, my_cold, my_hot).astype(f32)


def join_kernel(mine_ref, other_ref, out_ref):
    height = mine_ref.shape[0]
    out_ref[:height, :] = mine_ref[...]
    out_ref[height:, :] = other_ref[...]


def load_kernel(n, *refs):
    copies = []
    sems = refs[2 * n + 1]
    for index in range(n):
        src, dst = refs[index], refs[n + 1 + index]
        rows = src.shape[-2]
        parts = 4
        for part in range(parts):
            at = pl.ds(part * (rows // parts), rows // parts)
            lead = (0,) * (len(src.shape) - 2)
            if len(src.shape) == 4:
                for third in range(src.shape[1]):
                    copies.append((src.at[0, third, at], dst.at[0, third, at]))
            else:
                copies.append((src.at[lead + (at,)], dst.at[lead + (at,)]))
    started = []
    for number, (src, dst) in enumerate(copies):
        copy = pltpu.make_async_copy(src, dst, sems.at[number])
        copy.start()
        started.append(copy)
    for copy in started:
        copy.wait()


def routing(key_ref, meta, top, lanes):
    meta = meta.astype(jnp.float32)
    total = meta.shape[0]
    ids = meta[:, :top]
    gains = meta[:, top : 2 * top] + meta[:, 2 * top : 3 * top] + meta[:, 3 * top : 4 * top]
    is_cold = ids == key_ref[0:1, :top]
    is_hot = ids == key_ref[1:2, :top]
    cold_gain = jnp.sum(jnp.where(is_cold, gains, 0.0), axis=1, keepdims=True)
    hot_gain = jnp.sum(jnp.where(is_hot, gains, 0.0), axis=1, keepdims=True)
    mark = jnp.sum(jnp.where(is_cold, 1.0, 0.0), axis=1, keepdims=True)
    marks = jnp.broadcast_to(mark, (total, lanes))
    shape = (total, total)
    below = lax.broadcasted_iota(jnp.int32, shape, 0) > lax.broadcasted_iota(jnp.int32, shape, 1)
    rank = mm(jnp.where(below, 1.0, 0.0).astype(jnp.bfloat16), marks.astype(jnp.bfloat16))
    lane = lax.broadcasted_iota(jnp.int32, (total, lanes), 1).astype(jnp.float32)
    spread = jnp.where((marks > 0.5) & (rank == lane), 1.0, 0.0).astype(jnp.bfloat16)
    return cold_gain, hot_gain, spread


def load_rows(blocks, spans, x_ref):
    width, at, tails = x_ref.shape[1], 0, []
    for block, (first, size) in zip(blocks, spans):
        x_ref[at : at + size, :] = block[first : first + size, :width]
        tails.append(block[first : first + size, width : width + LANES])
        at += size
    return jnp.concatenate(tails, axis=0)


def weigh(hidden, packed_ref, spread, hot_ref, cold_gain, hot_gain, out_ref, first=0):
    width = out_ref.shape[1]
    rows = slice(first, first + hidden.shape[0])
    for start in range(0, width, STEP):
        at = slice(start, start + STEP)
        hot_part = mm(hidden, hot_ref[0, 2, :, at])
        cold_part = mm(spread, packed_ref[:, at])
        out_ref[rows, at] = (hot_gain * hot_part + cold_gain * cold_part).astype(out_ref.dtype)


def keep_gains(cold_gain, hot_gain, gain_ref):
    lane = lax.broadcasted_iota(jnp.int32, gain_ref.shape, 1)
    gain_ref[...] = jnp.where(lane == 0, cold_gain, hot_gain)


def early_kernel(spans, top, cap, key_ref, *refs):
    n = len(spans)
    hot_ref, hid_ref, pick_ref, spread_ref, gain_ref, x_ref = refs[n:]
    meta = load_rows(refs[:n], spans, x_ref)
    cold_gain, hot_gain, spread = routing(key_ref, meta, top, spread_ref.shape[1])
    spread_ref[...] = spread
    keep_gains(cold_gain, hot_gain, gain_ref)
    x = x_ref[...]
    hid_ref[...] = swish(mm(x, hot_ref[0, 0], NT), mm(x, hot_ref[0, 1], NT))
    pick_ref[...] = mm(spread[:, :cap], x, TN).astype(jnp.bfloat16)


def cold_expert(cold, gate_up_ref, down_ref, h_ref, packed_refs):
    units, width = down_ref.shape[1:]
    for start in range(0, units, STEP):
        gate = mm(cold, gate_up_ref[0, :, start : start + STEP])
        up = mm(cold, gate_up_ref[0, :, units + start : units + start + STEP])
        h_ref[:, start : start + STEP] = swish(gate, up)
    cold_hidden = h_ref[...]
    for start in range(0, width, STEP):
        at = slice(start, start + STEP)
        packed, end = mm(cold_hidden, down_ref[0, :, at]).astype(jnp.bfloat16), 0
        for packed_ref in packed_refs:
            packed_ref[:, at] = packed[end : end + packed_ref.shape[0]]
            end += packed_ref.shape[0]


def first_kernel(spans, top, cap, key_ref, *refs):
    n = len(spans)
    (gate_up_ref, down_ref, hot_ref), rest = refs[n : n + 3], refs[n + 3 :]
    hid_ref, packed_ref, spread_ref, gain_ref, x_ref, h_ref = rest
    meta = load_rows(refs[:n], spans, x_ref)
    cold_gain, hot_gain, spread = routing(key_ref, meta, top, spread_ref.shape[1])
    spread_ref[...] = spread
    keep_gains(cold_gain, hot_gain, gain_ref)
    x = x_ref[...]
    hid_ref[...] = swish(mm(x, hot_ref[0, 0], NT), mm(x, hot_ref[0, 1], NT))
    cold = mm(spread[:, :cap], x, TN).astype(jnp.bfloat16)
    cold_expert(cold, gate_up_ref, down_ref, h_ref, (packed_ref,))


def late_kernel(spans, top, cap, skip, key_ref, *refs):
    n = len(spans)
    (pick_ref, gate_up_ref, down_ref, hot_ref), rest = refs[n : n + 4], refs[n + 4 :]
    sib_ref, hid_ref, *packed_refs = rest[:4]
    spread_ref, gain_ref, x_ref, c_ref, h_ref = rest[4:]
    width = x_ref.shape[1]
    meta = load_rows(refs[:n], spans, x_ref)
    cold_gain, hot_gain, spread = routing(key_ref, meta, top, spread_ref.shape[1])
    spread_ref[...] = spread
    keep_gains(cold_gain, hot_gain, gain_ref)
    spread = spread[:, :cap]
    x = x_ref[...]
    n_picked = pick_ref.shape[0]
    c_ref[:n_picked, :] = pick_ref[...]
    c_ref[n_picked:, :] = mm(spread, x, TN).astype(jnp.bfloat16)
    cold_expert(c_ref[...], gate_up_ref, down_ref, h_ref, packed_refs)
    hidden = swish(mm(x, hot_ref[0, 0], NT), mm(x, hot_ref[0, 1], NT))
    hid_ref[...] = hidden
    weigh(
        hidden[skip:], packed_refs[1], spread[skip:], hot_ref, cold_gain[skip:], hot_gain[skip:], sib_ref
    )


def result_kernel(n_groups, jobs, hot_ref, *refs):
    outs = refs[4 * n_groups :]
    for group, first, size, out, place in jobs:
        hid_ref, packed_ref, spread_ref, gain_ref = refs[4 * group : 4 * group + 4]
        at = slice(first, first + size)
        weigh(
            hid_ref[at, :],
            packed_ref,
            spread_ref[at, : packed_ref.shape[0]],
            hot_ref,
            gain_ref[at, 0:1],
            gain_ref[at, 1:2],
            outs[out],
            place,
        )


def run_kernel(kernel, operands, outs, scratch, flops, moved, limit=12):
    vmem = pl.BlockSpec(memory_space=pltpu.VMEM)
    return pl.pallas_call(
        kernel,
        out_shape=[pltpu.VMEM(shape, dtype) for shape, dtype in outs],
        in_specs=[vmem] * len(operands),
        out_specs=[vmem] * len(outs),
        scratch_shapes=[pltpu.VMEM(shape, dtype) for shape, dtype in scratch],
        compiler_params=pltpu.CompilerParams(vmem_limit_bytes=limit * 2**20),
        cost_estimate=pl.CostEstimate(flops=flops, bytes_accessed=moved, transcendentals=0),
    )(*[pin(a) for a in operands])


def load_weights(weights, after):
    n = len(weights)
    hbm = lambda a: pltpu.with_memory_space_constraint(a, pltpu.HBM)
    return pl.pallas_call(
        functools.partial(load_kernel, n),
        out_shape=[pltpu.VMEM(w.shape, w.dtype) for w in weights],
        in_specs=[pl.BlockSpec(memory_space=pltpu.HBM)] * n + [pl.BlockSpec(memory_space=pl.ANY)],
        out_specs=[pl.BlockSpec(memory_space=pltpu.VMEM)] * n,
        scratch_shapes=[pltpu.SemaphoreType.DMA((4 * n + 8,))],
        compiler_params=pltpu.CompilerParams(vmem_limit_bytes=2**20),
        cost_estimate=pl.CostEstimate(
            flops=0, bytes_accessed=sum(w.size * 2 for w in weights), transcendentals=0
        ),
    )(*[hbm(w) for w in weights], after)


def make_message(hot_list, slot_of, tokens, ids, gains):
    rows, width = tokens.shape
    vmem, smem = pl.BlockSpec(memory_space=pltpu.VMEM), pl.BlockSpec(memory_space=pltpu.SMEM)
    hbm = lambda a: pltpu.with_memory_space_constraint(a, pltpu.HBM)
    return pl.pallas_call(
        message_kernel,
        out_shape=[
            pltpu.VMEM((rows, width + LANES), tokens.dtype),
            pltpu.VMEM((8, LANES), jnp.float32),
        ],
        in_specs=[smem] * 2 + [vmem] * 3,
        out_specs=[vmem] * 2,
        compiler_params=pltpu.CompilerParams(vmem_limit_bytes=2**21),
    )(*[hbm(a) for a in (hot_list, slot_of, tokens, ids, gains)])


def ring_perms(n_dp):
    chips = [(0, z) for z in range(n_dp)] + [(1, z) for z in reversed(range(n_dp))]
    size = len(chips)

    def device(place, core):
        x, z = chips[place % size]
        return (2 * x + core) * n_dp + z

    def hop(by, cross):
        return [
            (device(i, core), device(i + (-by if core else by), core ^ cross))
            for i in range(size)
            for core in range(2)
        ]

    swap = [(device(i, core), device(i, 1 - core)) for i in range(size) for core in range(2)]
    return hop, swap


def dense_body(tokens, expert_ids, route_w, hot_list, slot_of, cold_gate_up, cold_down, hot_weights):
    tok_rows, width = tokens.shape
    top = expert_ids.shape[1]
    n_hot, n_exp = hot_list.shape[0], slot_of.shape[0]
    n_dp = lax.axis_size("dp")
    units, hot_units = cold_down.shape[1], hot_weights.shape[3]
    cold_cap = -(-(tok_rows * top - n_hot * tok_rows) // (n_exp - n_hot))
    f32, bf16 = jnp.float32, jnp.bfloat16
    hop, swap_pairs = ring_perms(n_dp)
    axes = ("ep", "dp")
    move = lambda a, by: lax.ppermute(a, axes, hop(by, 0))
    cross = lambda a, by: lax.ppermute(a, axes, hop(by, 1))
    swap = lambda a: lax.ppermute(a, axes, swap_pairs)
    tie = lambda *arrays: lax.optimization_barrier(arrays)

    mine, key = make_message(hot_list, slot_of, tokens, expert_ids.T, route_w.T)
    (message,) = run_kernel(
        join_kernel, (mine, swap(mine)), [((2 * tok_rows, mine.shape[1]), bf16)], [], 0, 4 * mine.size, 2
    )
    weights = (cold_gate_up, cold_down, jnp.swapaxes(hot_weights, 2, 3))
    gate_up, down, hot = load_weights(weights, message)

    two = move(message, 2)
    later, hot = tie(message, hot)
    one = move(later, 1)
    two, hot = tie(two, hot)
    four, three = move(two[:tok_rows], 2), move(two, 1)

    sib_two = swap(two)
    whole, half, rest = (0, 2 * tok_rows), (0, tok_rows), (tok_rows, tok_rows)
    pad = lambda n: -(-n * cold_cap // 16) * 16
    lanes = lambda cap: -(-cap // LANES) * LANES

    def facts(spans):
        rows = sum(size for _, size in spans)
        cap = pad(rows // tok_rows)
        kept = [((rows, lanes(cap)), bf16), ((rows, LANES), f32)]
        return rows, cap, kept

    def early(blocks, spans):
        rows, cap, kept = facts(spans)
        return run_kernel(
            functools.partial(early_kernel, spans, top, cap),
            (key, *blocks, hot),
            [((rows, hot_units), bf16), ((cap, width), bf16), *kept],
            [((rows, width), bf16)],
            2 * rows * width * (2 * hot_units + cap),
            4 * rows * width,
        )

    spans = (whole, half, whole, rest, whole)
    rows, cap_a, kept = facts(spans)
    a_rows = run_kernel(
        functools.partial(first_kernel, spans, top, cap_a),
        (key, two, message, sib_two, message, one, gate_up, down, hot),
        [((rows, hot_units), bf16), ((cap_a, width), bf16), *kept],
        [((rows, width), bf16), ((cap_a, units), bf16)],
        2 * cap_a * 3 * units * width,
        4 * rows * width,
    )
    def results(groups, jobs, outs):
        size = sum(job[2] for job in jobs)
        return run_kernel(
            functools.partial(result_kernel, len(groups), jobs),
            (hot, *[a for group in groups for a in group]),
            outs,
            [],
            2 * size * width * (hot_units + cap_a),
            4 * size * width,
        )

    r = tok_rows
    back_a, mine = results(
        (a_rows,),
        (
            (0, 3 * r, 3 * r, 0, 0),
            (0, 0, 2 * r, 1, 0),
            (0, 6 * r, 2 * r, 1, 2 * r),
            (0, 2 * r, r, 1, 4 * r),
        ),
        [((3 * r, width), bf16), ((5 * r, width), f32)],
    )
    four, three, one, mine = tie(four, three, one, mine)
    sib_one, sib_four, sib_three = swap(one), swap(four), swap(three)
    hid_b, pick_b, *kept_b = early((four, three), (half, whole))
    spans = (whole, half, whole)
    rows, cap, kept = facts(spans)
    cap_b, skip = pick_b.shape[0], 2 * tok_rows
    back_late, hid_c, packed_b, packed_c, *kept_c = run_kernel(
        functools.partial(late_kernel, spans, top, cap, skip),
        (key, sib_one, sib_four, sib_three, pick_b, gate_up, down, hot),
        [
            ((rows - skip, width), bf16),
            ((rows, hot_units), bf16),
            ((cap_b, width), bf16),
            ((cap, width), bf16),
            *kept,
        ],
        [((rows, width), bf16), ((cap_b + cap, width), bf16), ((cap_b + cap, units), bf16)],
        2 * (cap_b + cap) * 3 * units * width,
        4 * rows * width,
    )
    b_rows = (hid_b, packed_b, *kept_b)
    c_rows = (hid_c, packed_c, *kept_c)
    low = lambda a: a.astype(bf16)
    from_late = swap(back_late)
    back_one, mine_late = results(
        (b_rows, c_rows),
        ((1, 0, 2 * r, 0, 0), (0, 0, 3 * r, 1, 0)),
        [((2 * r, width), bf16), ((3 * r, width), f32)],
    )
    from_a, from_one = swap(back_a).astype(f32), swap(back_one).astype(f32)
    late = mine_late + from_late.astype(f32)
    fourth, third = tie(low(late[:tok_rows]), low(late[tok_rows:]))
    fourth, third = move(fourth, -2).astype(f32), move(third, -1).astype(f32)
    far_sum = mine[: 2 * r] + from_a[: 2 * r]
    one_sum = mine[2 * r : 4 * r] + from_one
    own_sum = mine[4 * r :] + from_a[2 * r :]
    fourth, nearest = tie(fourth, low(one_sum))
    close = move(nearest, -1)
    far = tie(low(far_sum[:r] + third[:r] + fourth), low(far_sum[r:] + third[r:]))
    parts = (close[:tok_rows], swap(close[tok_rows:]), move(far[0], -2), cross(far[1], -2))
    return low(sum((a.astype(f32) for a in parts), own_sum))


def body(tokens, expert_ids, *rest):
    hot_list, slot_of = rest[1], rest[2]
    every_row_hot = 2 * expert_ids.shape[1] == slot_of.shape[0]
    two_columns = lax.axis_size("ep") == 4 and lax.axis_size("dp") == 4
    chosen = dense_body if every_row_hot and two_columns else routed_body
    return chosen(tokens, expert_ids, *rest)


def solution(mesh):
    in_specs = (
        P(("groups", "ep", "dp"), None),
        P(("groups", "ep", "dp"), None),
        P(("groups", "ep", "dp"), None),
        P("groups"),
        P(),
        P(("ep", "dp"), None, None),
        P(("ep", "dp"), None, None),
        P("dp", None, None, "ep"),
    )
    out_specs = P(("groups", "ep", "dp"), None)
    return jax.shard_map(body, mesh=mesh, in_specs=in_specs, out_specs=out_specs, check_vma=False)
```

```python
import functools

import jax
import jax.numpy as jnp
from jax import lax
from jax.experimental import pallas as pl
from jax.experimental.pallas import tpu as pltpu
from jax.sharding import PartitionSpec as P


def swiglu_rows(inputs, gate_up, down_proj):
    in_shape = inputs.shape
    flat_in = inputs.reshape(-1, in_shape[-1])
    hidden_width = down_proj.shape[0]
    both_out = jnp.dot(flat_in, gate_up, preferred_element_type=jnp.float32)
    hidden = (jax.nn.silu(both_out[:, :hidden_width]) * both_out[:, hidden_width:]).astype(
        jnp.bfloat16
    )
    result = jnp.dot(hidden, down_proj, preferred_element_type=jnp.float32)
    return result.astype(jnp.bfloat16).reshape(in_shape)


def sliced_rows(inputs, triple):
    in_shape = inputs.shape
    flat_in = inputs.reshape(-1, in_shape[-1])
    gate_out = jnp.dot(flat_in, triple[0], preferred_element_type=jnp.float32)
    up_out = jnp.dot(flat_in, triple[1], preferred_element_type=jnp.float32)
    hidden = (jax.nn.silu(gate_out) * up_out).astype(jnp.bfloat16)
    result = lax.dot_general(
        hidden, triple[2], (((1,), (1,)), ((), ())), preferred_element_type=jnp.float32
    )
    return result.reshape(in_shape)


def routed_body(tokens, expert_ids, route_w, hot_list, slot_of, cold_gate_up, cold_down, hot_weights):
    tok_rows, model_width = tokens.shape
    top_count = expert_ids.shape[1]
    n_hot = hot_list.shape[0]
    n_exp = slot_of.shape[0]
    n_ep = lax.axis_size("ep")
    n_dp = lax.axis_size("dp")
    n_dev = n_ep * n_dp
    most_rows = 2 * tok_rows * top_count // n_exp
    spare_rows = tok_rows * top_count - n_hot * most_rows
    cold_cap = (spare_rows + n_exp - n_hot - 1) // (n_exp - n_hot)
    one_hot = expert_ids[:, :, None] == jnp.arange(n_exp, dtype=jnp.int32)[None, None, :]
    slot_ids = jnp.sum(jnp.where(one_hot, slot_of[None, None, :], 0), axis=2)
    hot_match = expert_ids[:, :, None] == hot_list[None, None, :]
    is_hot = jnp.any(hot_match, axis=2)
    hot_index = jnp.sum(
        jnp.where(hot_match, jnp.arange(n_hot, dtype=jnp.int32)[None, None, :], 0), axis=2
    )
    flat_onehot = one_hot.reshape(tok_rows * top_count, n_exp).astype(jnp.int32)
    earlier = jnp.cumsum(flat_onehot, axis=0) - flat_onehot
    rank_ids = jnp.sum(earlier * flat_onehot, axis=1).reshape(tok_rows, top_count)
    row_ids = jnp.broadcast_to(
        jnp.arange(tok_rows, dtype=jnp.int32)[:, None], (tok_rows, top_count)
    ).reshape(-1)
    cold_size = n_dev * cold_cap
    hot_size = n_hot * most_rows
    cold_target = jnp.where(is_hot, cold_size, slot_ids * cold_cap + rank_ids).reshape(-1)
    hot_target = jnp.where(is_hot, hot_index * most_rows + rank_ids, hot_size).reshape(-1)
    cold_map = jnp.full((cold_size,), tok_rows, jnp.int32).at[cold_target].set(row_ids, mode="drop")
    hot_map = jnp.full((hot_size,), tok_rows, jnp.int32).at[hot_target].set(row_ids, mode="drop")
    padded = jnp.concatenate([tokens, jnp.zeros((1, model_width), tokens.dtype)], axis=0)
    cold_send = jnp.take(padded, cold_map, axis=0).reshape(n_dev, cold_cap, model_width)
    hot_send = jnp.take(padded, hot_map, axis=0).reshape(n_hot, most_rows, model_width)
    gate_up = cold_gate_up[0]
    down_proj = cold_down[0]
    cold_back = lax.all_to_all(
        swiglu_rows(
            lax.all_to_all(cold_send, ("ep", "dp"), split_axis=0, concat_axis=0, tiled=True),
            gate_up,
            down_proj,
        ),
        ("ep", "dp"),
        split_axis=0,
        concat_axis=0,
        tiled=True,
    )
    hot_recv = lax.all_to_all(hot_send, "dp", split_axis=0, concat_axis=0, tiled=True)
    gathered = lax.all_gather(hot_recv, "ep", axis=0, tiled=True)
    own_slice = hot_weights[0]
    hot_sum = lax.psum_scatter(
        sliced_rows(gathered, own_slice), "ep", scatter_dimension=0, tiled=True
    )
    hot_back = lax.all_to_all(
        hot_sum.astype(jnp.bfloat16), "dp", split_axis=0, concat_axis=0, tiled=True
    )
    answers = jnp.concatenate(
        [cold_back.reshape(cold_size, model_width), hot_back.reshape(hot_size, model_width)], axis=0
    )
    positions = jnp.where(
        is_hot, cold_size + hot_index * most_rows + rank_ids, slot_ids * cold_cap + rank_ids
    )
    picked = jnp.take(answers, positions, axis=0)
    mixed = jnp.zeros((tok_rows, model_width), jnp.float32)
    for column in range(top_count):
        mixed = mixed + route_w[:, column, None] * picked[:, column].astype(jnp.float32)
    return mixed.astype(jnp.bfloat16)


def pin(array):
    return pltpu.with_memory_space_constraint(array, pltpu.VMEM)


NN = (((1,), (0,)), ((), ()))
NT = (((1,), (1,)), ((), ()))
TN = (((0,), (0,)), ((), ()))
STEP = 256
LANES = 128


def mm(a, b, dims=NN):
    return lax.dot_general(a, b, dims, preferred_element_type=jnp.float32)


def swish(gate, up):
    return (gate / (1.0 + jnp.exp(-gate)) * up).astype(jnp.bfloat16)


def message_kernel(hot_list_ref, slot_ref, tok_ref, ids_ref, gain_ref, out_ref, key_ref):
    width = tok_ref.shape[1]
    out_ref[:, :width] = tok_ref[...]
    bf16, f32 = jnp.bfloat16, jnp.float32
    gains = gain_ref[...]
    terms = [ids_ref[...].astype(f32)]
    for _ in range(3):
        term = gains.astype(bf16).astype(f32)
        terms.append(term)
        gains = gains - term
    stacked = jnp.concatenate(terms, axis=0).astype(bf16)
    shape = (stacked.shape[0], LANES)
    row, lane = (lax.broadcasted_iota(jnp.int32, shape, axis) for axis in (0, 1))
    place = jnp.where(row == lane, 1.0, 0.0).astype(bf16)
    out_ref[:, width:] = mm(stacked, place, TN).astype(bf16)
    along = lax.axis_index("dp")
    me = lax.axis_index("ep") * lax.axis_size("dp") + along
    my_cold, my_hot = jnp.int32(0), jnp.int32(0)
    for expert in range(slot_ref.shape[0]):
        my_cold = jnp.where(slot_ref[expert] == me, expert, my_cold)
    held = my_cold
    for place in range(hot_list_ref.shape[0]):
        my_cold = jnp.where(hot_list_ref[place] == held, -1, my_cold)
        my_hot = jnp.where(along == place, hot_list_ref[place], my_hot)
    row = lax.broadcasted_iota(jnp.int32, key_ref.shape, 0)
    key_ref[...] = jnp.where(row == 0, my_cold, my_hot).astype(f32)


def join_kernel(mine_ref, other_ref, out_ref):
    height = mine_ref.shape[0]
    out_ref[:height, :] = mine_ref[...]
    out_ref[height:, :] = other_ref[...]


def load_kernel(n, *refs):
    copies = []
    sems = refs[2 * n + 1]
    for index in range(n):
        src, dst = refs[index], refs[n + 1 + index]
        rows = src.shape[-2]
        parts = 4
        for part in range(parts):
            at = pl.ds(part * (rows // parts), rows // parts)
            lead = (0,) * (len(src.shape) - 2)
            if len(src.shape) == 4:
                for third in range(src.shape[1]):
                    copies.append((src.at[0, third, at], dst.at[0, third, at]))
            else:
                copies.append((src.at[lead + (at,)], dst.at[lead + (at,)]))
    started = []
    for number, (src, dst) in enumerate(copies):
        copy = pltpu.make_async_copy(src, dst, sems.at[number])
        copy.start()
        started.append(copy)
    for copy in started:
        copy.wait()


def routing(key_ref, meta, top, lanes):
    meta = meta.astype(jnp.float32)
    total = meta.shape[0]
    ids = meta[:, :top]
    gains = meta[:, top : 2 * top] + meta[:, 2 * top : 3 * top] + meta[:, 3 * top : 4 * top]
    is_cold = ids == key_ref[0:1, :top]
    is_hot = ids == key_ref[1:2, :top]
    cold_gain = jnp.sum(jnp.where(is_cold, gains, 0.0), axis=1, keepdims=True)
    hot_gain = jnp.sum(jnp.where(is_hot, gains, 0.0), axis=1, keepdims=True)
    mark = jnp.sum(jnp.where(is_cold, 1.0, 0.0), axis=1, keepdims=True)
    marks = jnp.broadcast_to(mark, (total, lanes))
    shape = (total, total)
    below = lax.broadcasted_iota(jnp.int32, shape, 0) > lax.broadcasted_iota(jnp.int32, shape, 1)
    rank = mm(jnp.where(below, 1.0, 0.0).astype(jnp.bfloat16), marks.astype(jnp.bfloat16))
    lane = lax.broadcasted_iota(jnp.int32, (total, lanes), 1).astype(jnp.float32)
    spread = jnp.where((marks > 0.5) & (rank == lane), 1.0, 0.0).astype(jnp.bfloat16)
    return cold_gain, hot_gain, spread


def load_rows(blocks, spans, x_ref):
    width, at, tails = x_ref.shape[1], 0, []
    for block, (first, size) in zip(blocks, spans):
        x_ref[at : at + size, :] = block[first : first + size, :width]
        tails.append(block[first : first + size, width : width + LANES])
        at += size
    return jnp.concatenate(tails, axis=0)


def weigh(hidden, packed_ref, spread, hot_ref, cold_gain, hot_gain, out_ref, first=0):
    width = out_ref.shape[1]
    rows = slice(first, first + hidden.shape[0])
    for start in range(0, width, STEP):
        at = slice(start, start + STEP)
        hot_part = mm(hidden, hot_ref[0, 2, :, at])
        cold_part = mm(spread, packed_ref[:, at])
        out_ref[rows, at] = (hot_gain * hot_part + cold_gain * cold_part).astype(out_ref.dtype)


def keep_gains(cold_gain, hot_gain, gain_ref):
    lane = lax.broadcasted_iota(jnp.int32, gain_ref.shape, 1)
    gain_ref[...] = jnp.where(lane == 0, cold_gain, hot_gain)


def early_kernel(spans, top, cap, key_ref, *refs):
    n = len(spans)
    hot_ref, hid_ref, pick_ref, spread_ref, gain_ref, x_ref = refs[n:]
    meta = load_rows(refs[:n], spans, x_ref)
    cold_gain, hot_gain, spread = routing(key_ref, meta, top, spread_ref.shape[1])
    spread_ref[...] = spread
    keep_gains(cold_gain, hot_gain, gain_ref)
    x = x_ref[...]
    hid_ref[...] = swish(mm(x, hot_ref[0, 0], NT), mm(x, hot_ref[0, 1], NT))
    pick_ref[...] = mm(spread[:, :cap], x, TN).astype(jnp.bfloat16)


def cold_expert(cold, gate_up_ref, down_ref, h_ref, packed_refs):
    units, width = down_ref.shape[1:]
    for start in range(0, units, STEP):
        gate = mm(cold, gate_up_ref[0, :, start : start + STEP])
        up = mm(cold, gate_up_ref[0, :, units + start : units + start + STEP])
        h_ref[:, start : start + STEP] = swish(gate, up)
    cold_hidden = h_ref[...]
    for start in range(0, width, STEP):
        at = slice(start, start + STEP)
        packed, end = mm(cold_hidden, down_ref[0, :, at]).astype(jnp.bfloat16), 0
        for packed_ref in packed_refs:
            packed_ref[:, at] = packed[end : end + packed_ref.shape[0]]
            end += packed_ref.shape[0]


def first_kernel(spans, top, cap, key_ref, *refs):
    n = len(spans)
    (gate_up_ref, down_ref, hot_ref), rest = refs[n : n + 3], refs[n + 3 :]
    hid_ref, packed_ref, spread_ref, gain_ref, x_ref, h_ref = rest
    meta = load_rows(refs[:n], spans, x_ref)
    cold_gain, hot_gain, spread = routing(key_ref, meta, top, spread_ref.shape[1])
    spread_ref[...] = spread
    keep_gains(cold_gain, hot_gain, gain_ref)
    x = x_ref[...]
    hid_ref[...] = swish(mm(x, hot_ref[0, 0], NT), mm(x, hot_ref[0, 1], NT))
    cold = mm(spread[:, :cap], x, TN).astype(jnp.bfloat16)
    cold_expert(cold, gate_up_ref, down_ref, h_ref, (packed_ref,))


def late_kernel(spans, top, cap, skip, key_ref, *refs):
    n = len(spans)
    (pick_ref, gate_up_ref, down_ref, hot_ref), rest = refs[n : n + 4], refs[n + 4 :]
    sib_ref, hid_ref, *packed_refs = rest[:4]
    spread_ref, gain_ref, x_ref, c_ref, h_ref = rest[4:]
    width = x_ref.shape[1]
    meta = load_rows(refs[:n], spans, x_ref)
    cold_gain, hot_gain, spread = routing(key_ref, meta, top, spread_ref.shape[1])
    spread_ref[...] = spread
    keep_gains(cold_gain, hot_gain, gain_ref)
    spread = spread[:, :cap]
    x = x_ref[...]
    n_picked = pick_ref.shape[0]
    c_ref[:n_picked, :] = pick_ref[...]
    c_ref[n_picked:, :] = mm(spread, x, TN).astype(jnp.bfloat16)
    cold_expert(c_ref[...], gate_up_ref, down_ref, h_ref, packed_refs)
    hidden = swish(mm(x, hot_ref[0, 0], NT), mm(x, hot_ref[0, 1], NT))
    hid_ref[...] = hidden
    weigh(
        hidden[skip:], packed_refs[1], spread[skip:], hot_ref, cold_gain[skip:], hot_gain[skip:], sib_ref
    )


def result_kernel(n_groups, jobs, hot_ref, *refs):
    outs = refs[4 * n_groups :]
    for group, first, size, out, place in jobs:
        hid_ref, packed_ref, spread_ref, gain_ref = refs[4 * group : 4 * group + 4]
        at = slice(first, first + size)
        weigh(
            hid_ref[at, :],
            packed_ref,
            spread_ref[at, : packed_ref.shape[0]],
            hot_ref,
            gain_ref[at, 0:1],
            gain_ref[at, 1:2],
            outs[out],
            place,
        )


def run_kernel(kernel, operands, outs, scratch, flops, moved, limit=12):
    vmem = pl.BlockSpec(memory_space=pltpu.VMEM)
    return pl.pallas_call(
        kernel,
        out_shape=[pltpu.VMEM(shape, dtype) for shape, dtype in outs],
        in_specs=[vmem] * len(operands),
        out_specs=[vmem] * len(outs),
        scratch_shapes=[pltpu.VMEM(shape, dtype) for shape, dtype in scratch],
        compiler_params=pltpu.CompilerParams(vmem_limit_bytes=limit * 2**20),
        cost_estimate=pl.CostEstimate(flops=flops, bytes_accessed=moved, transcendentals=0),
    )(*[pin(a) for a in operands])


def load_weights(weights, after):
    n = len(weights)
    hbm = lambda a: pltpu.with_memory_space_constraint(a, pltpu.HBM)
    return pl.pallas_call(
        functools.partial(load_kernel, n),
        out_shape=[pltpu.VMEM(w.shape, w.dtype) for w in weights],
        in_specs=[pl.BlockSpec(memory_space=pltpu.HBM)] * n + [pl.BlockSpec(memory_space=pl.ANY)],
        out_specs=[pl.BlockSpec(memory_space=pltpu.VMEM)] * n,
        scratch_shapes=[pltpu.SemaphoreType.DMA((4 * n + 8,))],
        compiler_params=pltpu.CompilerParams(vmem_limit_bytes=2**20),
        cost_estimate=pl.CostEstimate(
            flops=0, bytes_accessed=sum(w.size * 2 for w in weights), transcendentals=0
        ),
    )(*[hbm(w) for w in weights], after)


def make_message(hot_list, slot_of, tokens, ids, gains):
    rows, width = tokens.shape
    vmem, smem = pl.BlockSpec(memory_space=pltpu.VMEM), pl.BlockSpec(memory_space=pltpu.SMEM)
    hbm = lambda a: pltpu.with_memory_space_constraint(a, pltpu.HBM)
    return pl.pallas_call(
        message_kernel,
        out_shape=[
            pltpu.VMEM((rows, width + LANES), tokens.dtype),
            pltpu.VMEM((8, LANES), jnp.float32),
        ],
        in_specs=[smem] * 2 + [vmem] * 3,
        out_specs=[vmem] * 2,
        compiler_params=pltpu.CompilerParams(vmem_limit_bytes=2**21),
    )(*[hbm(a) for a in (hot_list, slot_of, tokens, ids, gains)])


def ring_perms(n_dp):
    chips = [(0, z) for z in range(n_dp)] + [(1, z) for z in reversed(range(n_dp))]
    size = len(chips)

    def device(place, core):
        x, z = chips[place % size]
        return (2 * x + core) * n_dp + z

    def hop(by, cross):
        return [
            (device(i, core), device(i + (-by if core else by), core ^ cross))
            for i in range(size)
            for core in range(2)
        ]

    swap = [(device(i, core), device(i, 1 - core)) for i in range(size) for core in range(2)]
    return hop, swap


def dense_body(tokens, expert_ids, route_w, hot_list, slot_of, cold_gate_up, cold_down, hot_weights):
    tok_rows, width = tokens.shape
    top = expert_ids.shape[1]
    n_hot, n_exp = hot_list.shape[0], slot_of.shape[0]
    n_dp = lax.axis_size("dp")
    units, hot_units = cold_down.shape[1], hot_weights.shape[3]
    cold_cap = -(-(tok_rows * top - n_hot * tok_rows) // (n_exp - n_hot))
    f32, bf16 = jnp.float32, jnp.bfloat16
    hop, swap_pairs = ring_perms(n_dp)
    axes = ("ep", "dp")
    move = lambda a, by: lax.ppermute(a, axes, hop(by, 0))
    cross = lambda a, by: lax.ppermute(a, axes, hop(by, 1))
    swap = lambda a: lax.ppermute(a, axes, swap_pairs)
    tie = lambda *arrays: lax.optimization_barrier(arrays)

    mine, key = make_message(hot_list, slot_of, tokens, expert_ids.T, route_w.T)
    (message,) = run_kernel(
        join_kernel, (mine, swap(mine)), [((2 * tok_rows, mine.shape[1]), bf16)], [], 0, 4 * mine.size, 2
    )
    weights = (cold_gate_up, cold_down, jnp.swapaxes(hot_weights, 2, 3))
    gate_up, down, hot = load_weights(weights, message)

    two = move(message, 2)
    later, hot = tie(message, hot)
    one = move(later, 1)
    two, hot = tie(two, hot)
    four, three = move(two[:tok_rows], 2), move(two, 1)

    sib_two = swap(two)
    whole, half, rest = (0, 2 * tok_rows), (0, tok_rows), (tok_rows, tok_rows)
    pad = lambda n: -(-n * cold_cap // 16) * 16
    lanes = lambda cap: -(-cap // LANES) * LANES

    def facts(spans):
        rows = sum(size for _, size in spans)
        cap = pad(rows // tok_rows)
        kept = [((rows, lanes(cap)), bf16), ((rows, LANES), f32)]
        return rows, cap, kept

    def early(blocks, spans):
        rows, cap, kept = facts(spans)
        return run_kernel(
            functools.partial(early_kernel, spans, top, cap),
            (key, *blocks, hot),
            [((rows, hot_units), bf16), ((cap, width), bf16), *kept],
            [((rows, width), bf16)],
            2 * rows * width * (2 * hot_units + cap),
            4 * rows * width,
        )

    spans = (whole, half, whole, rest, whole)
    rows, cap_a, kept = facts(spans)
    a_rows = run_kernel(
        functools.partial(first_kernel, spans, top, cap_a),
        (key, two, message, sib_two, message, one, gate_up, down, hot),
        [((rows, hot_units), bf16), ((cap_a, width), bf16), *kept],
        [((rows, width), bf16), ((cap_a, units), bf16)],
        2 * cap_a * 3 * units * width,
        4 * rows * width,
    )
    def results(groups, jobs, outs):
        size = sum(job[2] for job in jobs)
        return run_kernel(
            functools.partial(result_kernel, len(groups), jobs),
            (hot, *[a for group in groups for a in group]),
            outs,
            [],
            2 * size * width * (hot_units + cap_a),
            4 * size * width,
        )

    r = tok_rows
    back_a, mine = results(
        (a_rows,),
        (
            (0, 3 * r, 3 * r, 0, 0),
            (0, 0, 2 * r, 1, 0),
            (0, 6 * r, 2 * r, 1, 2 * r),
            (0, 2 * r, r, 1, 4 * r),
        ),
        [((3 * r, width), bf16), ((5 * r, width), f32)],
    )
    four, three, one, mine = tie(four, three, one, mine)
    sib_one, sib_four, sib_three = swap(one), swap(four), swap(three)
    hid_b, pick_b, *kept_b = early((four, three), (half, whole))
    spans = (whole, half, whole)
    rows, cap, kept = facts(spans)
    cap_b, skip = pick_b.shape[0], 2 * tok_rows
    back_late, hid_c, packed_b, packed_c, *kept_c = run_kernel(
        functools.partial(late_kernel, spans, top, cap, skip),
        (key, sib_one, sib_four, sib_three, pick_b, gate_up, down, hot),
        [
            ((rows - skip, width), bf16),
            ((rows, hot_units), bf16),
            ((cap_b, width), bf16),
            ((cap, width), bf16),
            *kept,
        ],
        [((rows, width), bf16), ((cap_b + cap, width), bf16), ((cap_b + cap, units), bf16)],
        2 * (cap_b + cap) * 3 * units * width,
        4 * rows * width,
    )
    b_rows = (hid_b, packed_b, *kept_b)
    c_rows = (hid_c, packed_c, *kept_c)
    low = lambda a: a.astype(bf16)
    from_late = swap(back_late)
    back_one, mine_late = results(
        (b_rows, c_rows),
        ((1, 0, 2 * r, 0, 0), (0, 0, 3 * r, 1, 0)),
        [((2 * r, width), bf16), ((3 * r, width), f32)],
    )
    from_a, from_one = swap(back_a), swap(back_one)
    join = lambda a, b: low(a + b.astype(f32))
    fourth, third = join(mine_late[:r], from_late[:r]), join(mine_late[r:], from_late[r:])
    fourth, third = move(fourth, -2), move(third, -1)
    far_sum = mine[: 2 * r] + from_a[: 2 * r].astype(f32)
    one_sum = mine[2 * r : 4 * r] + from_one.astype(f32)
    own_sum = mine[4 * r :] + from_a[2 * r :].astype(f32)
    fourth, nearest = tie(fourth, low(one_sum))
    close = move(nearest, -1)
    far = tie(low(far_sum[:r] + third[:r].astype(f32) + fourth.astype(f32)), join(far_sum[r:], third[r:]))
    parts = (close[:tok_rows], swap(close[tok_rows:]), move(far[0], -2), cross(far[1], -2))
    return low(sum((a.astype(f32) for a in parts), own_sum))


def body(tokens, expert_ids, *rest):
    hot_list, slot_of = rest[1], rest[2]
    every_row_hot = 2 * expert_ids.shape[1] == slot_of.shape[0]
    two_columns = lax.axis_size("ep") == 4 and lax.axis_size("dp") == 4
    chosen = dense_body if every_row_hot and two_columns else routed_body
    return chosen(tokens, expert_ids, *rest)


def solution(mesh):
    in_specs = (
        P(("groups", "ep", "dp"), None),
        P(("groups", "ep", "dp"), None),
        P(("groups", "ep", "dp"), None),
        P("groups"),
        P(),
        P(("ep", "dp"), None, None),
        P(("ep", "dp"), None, None),
        P("dp", None, None, "ep"),
    )
    out_specs = P(("groups", "ep", "dp"), None)
    return jax.shard_map(body, mesh=mesh, in_specs=in_specs, out_specs=out_specs, check_vma=False)
```

```python
import functools

import jax
import jax.numpy as jnp
from jax import lax
from jax.experimental import pallas as pl
from jax.experimental.pallas import tpu as pltpu
from jax.sharding import PartitionSpec as P


def swiglu_rows(inputs, gate_up, down_proj):
    in_shape = inputs.shape
    flat_in = inputs.reshape(-1, in_shape[-1])
    hidden_width = down_proj.shape[0]
    both_out = jnp.dot(flat_in, gate_up, preferred_element_type=jnp.float32)
    hidden = (jax.nn.silu(both_out[:, :hidden_width]) * both_out[:, hidden_width:]).astype(
        jnp.bfloat16
    )
    result = jnp.dot(hidden, down_proj, preferred_element_type=jnp.float32)
    return result.astype(jnp.bfloat16).reshape(in_shape)


def sliced_rows(inputs, triple):
    in_shape = inputs.shape
    flat_in = inputs.reshape(-1, in_shape[-1])
    gate_out = jnp.dot(flat_in, triple[0], preferred_element_type=jnp.float32)
    up_out = jnp.dot(flat_in, triple[1], preferred_element_type=jnp.float32)
    hidden = (jax.nn.silu(gate_out) * up_out).astype(jnp.bfloat16)
    result = lax.dot_general(
        hidden, triple[2], (((1,), (1,)), ((), ())), preferred_element_type=jnp.float32
    )
    return result.reshape(in_shape)


def routed_body(tokens, expert_ids, route_w, hot_list, slot_of, cold_gate_up, cold_down, hot_weights):
    tok_rows, model_width = tokens.shape
    top_count = expert_ids.shape[1]
    n_hot = hot_list.shape[0]
    n_exp = slot_of.shape[0]
    n_ep = lax.axis_size("ep")
    n_dp = lax.axis_size("dp")
    n_dev = n_ep * n_dp
    most_rows = 2 * tok_rows * top_count // n_exp
    spare_rows = tok_rows * top_count - n_hot * most_rows
    cold_cap = (spare_rows + n_exp - n_hot - 1) // (n_exp - n_hot)
    one_hot = expert_ids[:, :, None] == jnp.arange(n_exp, dtype=jnp.int32)[None, None, :]
    slot_ids = jnp.sum(jnp.where(one_hot, slot_of[None, None, :], 0), axis=2)
    hot_match = expert_ids[:, :, None] == hot_list[None, None, :]
    is_hot = jnp.any(hot_match, axis=2)
    hot_index = jnp.sum(
        jnp.where(hot_match, jnp.arange(n_hot, dtype=jnp.int32)[None, None, :], 0), axis=2
    )
    flat_onehot = one_hot.reshape(tok_rows * top_count, n_exp).astype(jnp.int32)
    earlier = jnp.cumsum(flat_onehot, axis=0) - flat_onehot
    rank_ids = jnp.sum(earlier * flat_onehot, axis=1).reshape(tok_rows, top_count)
    row_ids = jnp.broadcast_to(
        jnp.arange(tok_rows, dtype=jnp.int32)[:, None], (tok_rows, top_count)
    ).reshape(-1)
    cold_size = n_dev * cold_cap
    hot_size = n_hot * most_rows
    cold_target = jnp.where(is_hot, cold_size, slot_ids * cold_cap + rank_ids).reshape(-1)
    hot_target = jnp.where(is_hot, hot_index * most_rows + rank_ids, hot_size).reshape(-1)
    cold_map = jnp.full((cold_size,), tok_rows, jnp.int32).at[cold_target].set(row_ids, mode="drop")
    hot_map = jnp.full((hot_size,), tok_rows, jnp.int32).at[hot_target].set(row_ids, mode="drop")
    padded = jnp.concatenate([tokens, jnp.zeros((1, model_width), tokens.dtype)], axis=0)
    cold_send = jnp.take(padded, cold_map, axis=0).reshape(n_dev, cold_cap, model_width)
    hot_send = jnp.take(padded, hot_map, axis=0).reshape(n_hot, most_rows, model_width)
    gate_up = cold_gate_up[0]
    down_proj = cold_down[0]
    cold_back = lax.all_to_all(
        swiglu_rows(
            lax.all_to_all(cold_send, ("ep", "dp"), split_axis=0, concat_axis=0, tiled=True),
            gate_up,
            down_proj,
        ),
        ("ep", "dp"),
        split_axis=0,
        concat_axis=0,
        tiled=True,
    )
    hot_recv = lax.all_to_all(hot_send, "dp", split_axis=0, concat_axis=0, tiled=True)
    gathered = lax.all_gather(hot_recv, "ep", axis=0, tiled=True)
    own_slice = hot_weights[0]
    hot_sum = lax.psum_scatter(
        sliced_rows(gathered, own_slice), "ep", scatter_dimension=0, tiled=True
    )
    hot_back = lax.all_to_all(
        hot_sum.astype(jnp.bfloat16), "dp", split_axis=0, concat_axis=0, tiled=True
    )
    answers = jnp.concatenate(
        [cold_back.reshape(cold_size, model_width), hot_back.reshape(hot_size, model_width)], axis=0
    )
    positions = jnp.where(
        is_hot, cold_size + hot_index * most_rows + rank_ids, slot_ids * cold_cap + rank_ids
    )
    picked = jnp.take(answers, positions, axis=0)
    mixed = jnp.zeros((tok_rows, model_width), jnp.float32)
    for column in range(top_count):
        mixed = mixed + route_w[:, column, None] * picked[:, column].astype(jnp.float32)
    return mixed.astype(jnp.bfloat16)


def pin(array):
    return pltpu.with_memory_space_constraint(array, pltpu.VMEM)


NN = (((1,), (0,)), ((), ()))
NT = (((1,), (1,)), ((), ()))
TN = (((0,), (0,)), ((), ()))
STEP = 256
LANES = 128


def mm(a, b, dims=NN):
    return lax.dot_general(a, b, dims, preferred_element_type=jnp.float32)


def swish(gate, up):
    return (gate / (1.0 + jnp.exp(-gate)) * up).astype(jnp.bfloat16)


def message_kernel(hot_list_ref, slot_ref, tok_ref, ids_ref, gain_ref, out_ref, key_ref):
    width = tok_ref.shape[1]
    out_ref[:, :width] = tok_ref[...]
    bf16, f32 = jnp.bfloat16, jnp.float32
    gains = gain_ref[...]
    terms = [ids_ref[...].astype(f32)]
    for _ in range(3):
        term = gains.astype(bf16).astype(f32)
        terms.append(term)
        gains = gains - term
    stacked = jnp.concatenate(terms, axis=0).astype(bf16)
    shape = (stacked.shape[0], LANES)
    row, lane = (lax.broadcasted_iota(jnp.int32, shape, axis) for axis in (0, 1))
    place = jnp.where(row == lane, 1.0, 0.0).astype(bf16)
    out_ref[:, width:] = mm(stacked, place, TN).astype(bf16)
    along = lax.axis_index("dp")
    me = lax.axis_index("ep") * lax.axis_size("dp") + along
    my_cold, my_hot = jnp.int32(0), jnp.int32(0)
    for expert in range(slot_ref.shape[0]):
        my_cold = jnp.where(slot_ref[expert] == me, expert, my_cold)
    held = my_cold
    for place in range(hot_list_ref.shape[0]):
        my_cold = jnp.where(hot_list_ref[place] == held, -1, my_cold)
        my_hot = jnp.where(along == place, hot_list_ref[place], my_hot)
    row = lax.broadcasted_iota(jnp.int32, key_ref.shape, 0)
    key_ref[...] = jnp.where(row == 0, my_cold, my_hot).astype(f32)


def join_kernel(mine_ref, other_ref, out_ref):
    height = mine_ref.shape[0]
    out_ref[:height, :] = mine_ref[...]
    out_ref[height:, :] = other_ref[...]


def load_kernel(n, *refs):
    copies = []
    sems = refs[2 * n + 1]
    for index in range(n):
        src, dst = refs[index], refs[n + 1 + index]
        rows = src.shape[-2]
        parts = 4
        for part in range(parts):
            at = pl.ds(part * (rows // parts), rows // parts)
            lead = (0,) * (len(src.shape) - 2)
            if len(src.shape) == 4:
                for third in range(src.shape[1]):
                    copies.append((src.at[0, third, at], dst.at[0, third, at]))
            else:
                copies.append((src.at[lead + (at,)], dst.at[lead + (at,)]))
    started = []
    for number, (src, dst) in enumerate(copies):
        copy = pltpu.make_async_copy(src, dst, sems.at[number])
        copy.start()
        started.append(copy)
    for copy in started:
        copy.wait()


def routing(key_ref, meta, top, lanes):
    meta = meta.astype(jnp.float32)
    total = meta.shape[0]
    ids = meta[:, :top]
    gains = meta[:, top : 2 * top] + meta[:, 2 * top : 3 * top] + meta[:, 3 * top : 4 * top]
    is_cold = ids == key_ref[0:1, :top]
    is_hot = ids == key_ref[1:2, :top]
    cold_gain = jnp.sum(jnp.where(is_cold, gains, 0.0), axis=1, keepdims=True)
    hot_gain = jnp.sum(jnp.where(is_hot, gains, 0.0), axis=1, keepdims=True)
    mark = jnp.sum(jnp.where(is_cold, 1.0, 0.0), axis=1, keepdims=True)
    marks = jnp.broadcast_to(mark, (total, lanes))
    shape = (total, total)
    below = lax.broadcasted_iota(jnp.int32, shape, 0) > lax.broadcasted_iota(jnp.int32, shape, 1)
    rank = mm(jnp.where(below, 1.0, 0.0).astype(jnp.bfloat16), marks.astype(jnp.bfloat16))
    lane = lax.broadcasted_iota(jnp.int32, (total, lanes), 1).astype(jnp.float32)
    spread = jnp.where((marks > 0.5) & (rank == lane), 1.0, 0.0).astype(jnp.bfloat16)
    return cold_gain, hot_gain, spread


def load_rows(blocks, spans, x_ref):
    width, at, tails = x_ref.shape[1], 0, []
    for block, (first, size) in zip(blocks, spans):
        x_ref[at : at + size, :] = block[first : first + size, :width]
        tails.append(block[first : first + size, width : width + LANES])
        at += size
    return jnp.concatenate(tails, axis=0)


def weigh(hidden, packed_ref, spread, hot_ref, cold_gain, hot_gain, out_ref, first=0):
    width = out_ref.shape[1]
    rows = slice(first, first + hidden.shape[0])
    for start in range(0, width, STEP):
        at = slice(start, start + STEP)
        hot_part = mm(hidden, hot_ref[0, 2, :, at])
        cold_part = mm(spread, packed_ref[:, at])
        out_ref[rows, at] = (hot_gain * hot_part + cold_gain * cold_part).astype(out_ref.dtype)


def keep_gains(cold_gain, hot_gain, gain_ref):
    lane = lax.broadcasted_iota(jnp.int32, gain_ref.shape, 1)
    gain_ref[...] = jnp.where(lane == 0, cold_gain, hot_gain)


def early_kernel(spans, top, cap, key_ref, *refs):
    n = len(spans)
    hot_ref, hid_ref, pick_ref, spread_ref, gain_ref, x_ref = refs[n:]
    meta = load_rows(refs[:n], spans, x_ref)
    cold_gain, hot_gain, spread = routing(key_ref, meta, top, spread_ref.shape[1])
    spread_ref[...] = spread
    keep_gains(cold_gain, hot_gain, gain_ref)
    x = x_ref[...]
    hid_ref[...] = swish(mm(x, hot_ref[0, 0], NT), mm(x, hot_ref[0, 1], NT))
    pick_ref[...] = mm(spread[:, :cap], x, TN).astype(jnp.bfloat16)


def cold_expert(cold, gate_up_ref, down_ref, h_ref, packed_refs):
    units, width = down_ref.shape[1:]
    for start in range(0, units, STEP):
        gate = mm(cold, gate_up_ref[0, :, start : start + STEP])
        up = mm(cold, gate_up_ref[0, :, units + start : units + start + STEP])
        h_ref[:, start : start + STEP] = swish(gate, up)
    cold_hidden = h_ref[...]
    for start in range(0, width, STEP):
        at = slice(start, start + STEP)
        packed, end = mm(cold_hidden, down_ref[0, :, at]).astype(jnp.bfloat16), 0
        for packed_ref in packed_refs:
            packed_ref[:, at] = packed[end : end + packed_ref.shape[0]]
            end += packed_ref.shape[0]


def first_kernel(spans, top, cap, key_ref, *refs):
    n = len(spans)
    (gate_up_ref, down_ref, hot_ref), rest = refs[n : n + 3], refs[n + 3 :]
    hid_ref, packed_ref, spread_ref, gain_ref, x_ref, h_ref = rest
    meta = load_rows(refs[:n], spans, x_ref)
    cold_gain, hot_gain, spread = routing(key_ref, meta, top, spread_ref.shape[1])
    spread_ref[...] = spread
    keep_gains(cold_gain, hot_gain, gain_ref)
    x = x_ref[...]
    hid_ref[...] = swish(mm(x, hot_ref[0, 0], NT), mm(x, hot_ref[0, 1], NT))
    cold = mm(spread[:, :cap], x, TN).astype(jnp.bfloat16)
    cold_expert(cold, gate_up_ref, down_ref, h_ref, (packed_ref,))


def late_kernel(spans, top, cap, skip, key_ref, *refs):
    n = len(spans)
    (pick_ref, gate_up_ref, down_ref, hot_ref), rest = refs[n : n + 4], refs[n + 4 :]
    sib_ref, hid_ref, *packed_refs = rest[:4]
    spread_ref, gain_ref, x_ref, c_ref, h_ref = rest[4:]
    width = x_ref.shape[1]
    meta = load_rows(refs[:n], spans, x_ref)
    cold_gain, hot_gain, spread = routing(key_ref, meta, top, spread_ref.shape[1])
    spread_ref[...] = spread
    keep_gains(cold_gain, hot_gain, gain_ref)
    spread = spread[:, :cap]
    x = x_ref[...]
    n_picked = pick_ref.shape[0]
    c_ref[:n_picked, :] = pick_ref[...]
    c_ref[n_picked:, :] = mm(spread, x, TN).astype(jnp.bfloat16)
    cold_expert(c_ref[...], gate_up_ref, down_ref, h_ref, packed_refs)
    hidden = swish(mm(x, hot_ref[0, 0], NT), mm(x, hot_ref[0, 1], NT))
    hid_ref[...] = hidden
    weigh(
        hidden[skip:], packed_refs[1], spread[skip:], hot_ref, cold_gain[skip:], hot_gain[skip:], sib_ref
    )


def result_kernel(n_groups, jobs, hot_ref, *refs):
    outs = refs[4 * n_groups :]
    for group, first, size, out, place in jobs:
        hid_ref, packed_ref, spread_ref, gain_ref = refs[4 * group : 4 * group + 4]
        at = slice(first, first + size)
        weigh(
            hid_ref[at, :],
            packed_ref,
            spread_ref[at, : packed_ref.shape[0]],
            hot_ref,
            gain_ref[at, 0:1],
            gain_ref[at, 1:2],
            outs[out],
            place,
        )


def run_kernel(kernel, operands, outs, scratch, flops, moved, limit=12):
    vmem = pl.BlockSpec(memory_space=pltpu.VMEM)
    return pl.pallas_call(
        kernel,
        out_shape=[pltpu.VMEM(shape, dtype) for shape, dtype in outs],
        in_specs=[vmem] * len(operands),
        out_specs=[vmem] * len(outs),
        scratch_shapes=[pltpu.VMEM(shape, dtype) for shape, dtype in scratch],
        compiler_params=pltpu.CompilerParams(vmem_limit_bytes=limit * 2**20),
        cost_estimate=pl.CostEstimate(flops=flops, bytes_accessed=moved, transcendentals=0),
    )(*[pin(a) for a in operands])


def load_weights(weights, after):
    n = len(weights)
    hbm = lambda a: pltpu.with_memory_space_constraint(a, pltpu.HBM)
    return pl.pallas_call(
        functools.partial(load_kernel, n),
        out_shape=[pltpu.VMEM(w.shape, w.dtype) for w in weights],
        in_specs=[pl.BlockSpec(memory_space=pltpu.HBM)] * n + [pl.BlockSpec(memory_space=pl.ANY)],
        out_specs=[pl.BlockSpec(memory_space=pltpu.VMEM)] * n,
        scratch_shapes=[pltpu.SemaphoreType.DMA((4 * n + 8,))],
        compiler_params=pltpu.CompilerParams(vmem_limit_bytes=2**20),
        cost_estimate=pl.CostEstimate(
            flops=0, bytes_accessed=sum(w.size * 2 for w in weights), transcendentals=0
        ),
    )(*[hbm(w) for w in weights], after)


def make_message(hot_list, slot_of, tokens, ids, gains):
    rows, width = tokens.shape
    vmem, smem = pl.BlockSpec(memory_space=pltpu.VMEM), pl.BlockSpec(memory_space=pltpu.SMEM)
    hbm = lambda a: pltpu.with_memory_space_constraint(a, pltpu.HBM)
    return pl.pallas_call(
        message_kernel,
        out_shape=[
            pltpu.VMEM((rows, width + LANES), tokens.dtype),
            pltpu.VMEM((8, LANES), jnp.float32),
        ],
        in_specs=[smem] * 2 + [vmem] * 3,
        out_specs=[vmem] * 2,
        compiler_params=pltpu.CompilerParams(vmem_limit_bytes=2**21),
    )(*[hbm(a) for a in (hot_list, slot_of, tokens, ids, gains)])


def ring_perms(n_dp):
    chips = [(0, z) for z in range(n_dp)] + [(1, z) for z in reversed(range(n_dp))]
    size = len(chips)

    def device(place, core):
        x, z = chips[place % size]
        return (2 * x + core) * n_dp + z

    def hop(by, cross):
        return [
            (device(i, core), device(i + (-by if core else by), core ^ cross))
            for i in range(size)
            for core in range(2)
        ]

    swap = [(device(i, core), device(i, 1 - core)) for i in range(size) for core in range(2)]
    return hop, swap


def dense_body(tokens, expert_ids, route_w, hot_list, slot_of, cold_gate_up, cold_down, hot_weights):
    tok_rows, width = tokens.shape
    top = expert_ids.shape[1]
    n_hot, n_exp = hot_list.shape[0], slot_of.shape[0]
    n_dp = lax.axis_size("dp")
    units, hot_units = cold_down.shape[1], hot_weights.shape[3]
    cold_cap = -(-(tok_rows * top - n_hot * tok_rows) // (n_exp - n_hot))
    f32, bf16 = jnp.float32, jnp.bfloat16
    hop, swap_pairs = ring_perms(n_dp)
    axes = ("ep", "dp")
    move = lambda a, by: lax.ppermute(a, axes, hop(by, 0))
    cross = lambda a, by: lax.ppermute(a, axes, hop(by, 1))
    swap = lambda a: lax.ppermute(a, axes, swap_pairs)
    tie = lambda *arrays: lax.optimization_barrier(arrays)

    mine, key = make_message(hot_list, slot_of, tokens, expert_ids.T, route_w.T)
    (message,) = run_kernel(
        join_kernel, (mine, swap(mine)), [((2 * tok_rows, mine.shape[1]), bf16)], [], 0, 4 * mine.size, 2
    )
    weights = (cold_gate_up, cold_down, jnp.swapaxes(hot_weights, 2, 3))
    gate_up, down, hot = load_weights(weights, message)

    two = move(message, 2)
    later, hot = tie(message, hot)
    one = move(later, 1)
    two, hot = tie(two, hot)
    four, three = move(two[:tok_rows], 2), move(two, 1)

    sib_two = swap(two)
    whole, half, rest = (0, 2 * tok_rows), (0, tok_rows), (tok_rows, tok_rows)
    pad = lambda n: -(-n * cold_cap // 16) * 16
    lanes = lambda cap: -(-cap // LANES) * LANES

    def facts(spans):
        rows = sum(size for _, size in spans)
        cap = pad(rows // tok_rows)
        kept = [((rows, lanes(cap)), bf16), ((rows, LANES), f32)]
        return rows, cap, kept

    def early(blocks, spans):
        rows, cap, kept = facts(spans)
        return run_kernel(
            functools.partial(early_kernel, spans, top, cap),
            (key, *blocks, hot),
            [((rows, hot_units), bf16), ((cap, width), bf16), *kept],
            [((rows, width), bf16)],
            2 * rows * width * (2 * hot_units + cap),
            4 * rows * width,
        )

    spans = (whole, half, whole, rest, whole)
    rows, cap_a, kept = facts(spans)
    a_rows = run_kernel(
        functools.partial(first_kernel, spans, top, cap_a),
        (key, two, message, sib_two, message, one, gate_up, down, hot),
        [((rows, hot_units), bf16), ((cap_a, width), bf16), *kept],
        [((rows, width), bf16), ((cap_a, units), bf16)],
        2 * cap_a * 3 * units * width,
        4 * rows * width,
    )
    def results(groups, jobs, outs):
        size = sum(job[2] for job in jobs)
        return run_kernel(
            functools.partial(result_kernel, len(groups), jobs),
            (hot, *[a for group in groups for a in group]),
            outs,
            [],
            2 * size * width * (hot_units + cap_a),
            4 * size * width,
        )

    r = tok_rows
    back_a, mine = results(
        (a_rows,),
        (
            (0, 3 * r, 3 * r, 0, 0),
            (0, 0, 2 * r, 1, 0),
            (0, 6 * r, 2 * r, 1, 2 * r),
            (0, 2 * r, r, 1, 4 * r),
        ),
        [((3 * r, width), bf16), ((5 * r, width), f32)],
    )
    four, three, one, mine = tie(four, three, one, mine)
    sib_one, sib_four, sib_three = swap(one), swap(four), swap(three)
    hid_b, pick_b, *kept_b = early((four, three), (half, whole))
    spans = (whole, half, whole)
    rows, cap, kept = facts(spans)
    cap_b, skip = pick_b.shape[0], 2 * tok_rows
    back_late, hid_c, packed_b, packed_c, *kept_c = run_kernel(
        functools.partial(late_kernel, spans, top, cap, skip),
        (key, sib_one, sib_four, sib_three, pick_b, gate_up, down, hot),
        [
            ((rows - skip, width), bf16),
            ((rows, hot_units), bf16),
            ((cap_b, width), bf16),
            ((cap, width), bf16),
            *kept,
        ],
        [((rows, width), bf16), ((cap_b + cap, width), bf16), ((cap_b + cap, units), bf16)],
        2 * (cap_b + cap) * 3 * units * width,
        4 * rows * width,
    )
    b_rows = (hid_b, packed_b, *kept_b)
    c_rows = (hid_c, packed_c, *kept_c)
    low = lambda a: a.astype(bf16)
    from_late = swap(back_late)
    back_one, mine_late = results(
        (b_rows, c_rows),
        ((1, 0, 2 * r, 0, 0), (0, 0, 3 * r, 1, 0)),
        [((2 * r, width), bf16), ((3 * r, width), f32)],
    )
    from_a, from_one = swap(back_a), swap(back_one)
    join = lambda a, b: low(a + b.astype(f32))
    fourth, third = join(mine_late[:r], from_late[:r]), join(mine_late[r:], from_late[r:])
    fourth, third = move(fourth, -2), move(third, -1)
    far_sum = mine[: 2 * r] + from_a[: 2 * r].astype(f32)
    one_sum = mine[2 * r : 4 * r] + from_one.astype(f32)
    own_sum = mine[4 * r :] + from_a[2 * r :].astype(f32)
    fourth, nearest = tie(fourth, low(one_sum))
    close = move(nearest, -1)
    far = tie(low(far_sum[:r] + third[:r].astype(f32) + fourth.astype(f32)), join(far_sum[r:], third[r:]))
    crossed = cross(far[1], -2)
    parts = (close[:tok_rows], swap(close[tok_rows:]), crossed, move(far[0], -2))
    return low(sum((a.astype(f32) for a in parts), own_sum))


def body(tokens, expert_ids, *rest):
    hot_list, slot_of = rest[1], rest[2]
    every_row_hot = 2 * expert_ids.shape[1] == slot_of.shape[0]
    two_columns = lax.axis_size("ep") == 4 and lax.axis_size("dp") == 4
    chosen = dense_body if every_row_hot and two_columns else routed_body
    return chosen(tokens, expert_ids, *rest)


def solution(mesh):
    in_specs = (
        P(("groups", "ep", "dp"), None),
        P(("groups", "ep", "dp"), None),
        P(("groups", "ep", "dp"), None),
        P("groups"),
        P(),
        P(("ep", "dp"), None, None),
        P(("ep", "dp"), None, None),
        P("dp", None, None, "ep"),
    )
    out_specs = P(("groups", "ep", "dp"), None)
    return jax.shard_map(body, mesh=mesh, in_specs=in_specs, out_specs=out_specs, check_vma=False)
```

```python
import functools

import jax
import jax.numpy as jnp
from jax import lax
from jax.experimental import pallas as pl
from jax.experimental.pallas import tpu as pltpu
from jax.sharding import PartitionSpec as P


def swiglu_rows(inputs, gate_up, down_proj):
    in_shape = inputs.shape
    flat_in = inputs.reshape(-1, in_shape[-1])
    hidden_width = down_proj.shape[0]
    both_out = jnp.dot(flat_in, gate_up, preferred_element_type=jnp.float32)
    hidden = (jax.nn.silu(both_out[:, :hidden_width]) * both_out[:, hidden_width:]).astype(
        jnp.bfloat16
    )
    result = jnp.dot(hidden, down_proj, preferred_element_type=jnp.float32)
    return result.astype(jnp.bfloat16).reshape(in_shape)


def sliced_rows(inputs, triple):
    in_shape = inputs.shape
    flat_in = inputs.reshape(-1, in_shape[-1])
    gate_out = jnp.dot(flat_in, triple[0], preferred_element_type=jnp.float32)
    up_out = jnp.dot(flat_in, triple[1], preferred_element_type=jnp.float32)
    hidden = (jax.nn.silu(gate_out) * up_out).astype(jnp.bfloat16)
    result = lax.dot_general(
        hidden, triple[2], (((1,), (1,)), ((), ())), preferred_element_type=jnp.float32
    )
    return result.reshape(in_shape)


def routed_body(tokens, expert_ids, route_w, hot_list, slot_of, cold_gate_up, cold_down, hot_weights):
    tok_rows, model_width = tokens.shape
    top_count = expert_ids.shape[1]
    n_hot = hot_list.shape[0]
    n_exp = slot_of.shape[0]
    n_ep = lax.axis_size("ep")
    n_dp = lax.axis_size("dp")
    n_dev = n_ep * n_dp
    most_rows = 2 * tok_rows * top_count // n_exp
    spare_rows = tok_rows * top_count - n_hot * most_rows
    cold_cap = (spare_rows + n_exp - n_hot - 1) // (n_exp - n_hot)
    one_hot = expert_ids[:, :, None] == jnp.arange(n_exp, dtype=jnp.int32)[None, None, :]
    slot_ids = jnp.sum(jnp.where(one_hot, slot_of[None, None, :], 0), axis=2)
    hot_match = expert_ids[:, :, None] == hot_list[None, None, :]
    is_hot = jnp.any(hot_match, axis=2)
    hot_index = jnp.sum(
        jnp.where(hot_match, jnp.arange(n_hot, dtype=jnp.int32)[None, None, :], 0), axis=2
    )
    flat_onehot = one_hot.reshape(tok_rows * top_count, n_exp).astype(jnp.int32)
    earlier = jnp.cumsum(flat_onehot, axis=0) - flat_onehot
    rank_ids = jnp.sum(earlier * flat_onehot, axis=1).reshape(tok_rows, top_count)
    row_ids = jnp.broadcast_to(
        jnp.arange(tok_rows, dtype=jnp.int32)[:, None], (tok_rows, top_count)
    ).reshape(-1)
    cold_size = n_dev * cold_cap
    hot_size = n_hot * most_rows
    cold_target = jnp.where(is_hot, cold_size, slot_ids * cold_cap + rank_ids).reshape(-1)
    hot_target = jnp.where(is_hot, hot_index * most_rows + rank_ids, hot_size).reshape(-1)
    cold_map = jnp.full((cold_size,), tok_rows, jnp.int32).at[cold_target].set(row_ids, mode="drop")
    hot_map = jnp.full((hot_size,), tok_rows, jnp.int32).at[hot_target].set(row_ids, mode="drop")
    padded = jnp.concatenate([tokens, jnp.zeros((1, model_width), tokens.dtype)], axis=0)
    cold_send = jnp.take(padded, cold_map, axis=0).reshape(n_dev, cold_cap, model_width)
    hot_send = jnp.take(padded, hot_map, axis=0).reshape(n_hot, most_rows, model_width)
    gate_up = cold_gate_up[0]
    down_proj = cold_down[0]
    cold_back = lax.all_to_all(
        swiglu_rows(
            lax.all_to_all(cold_send, ("ep", "dp"), split_axis=0, concat_axis=0, tiled=True),
            gate_up,
            down_proj,
        ),
        ("ep", "dp"),
        split_axis=0,
        concat_axis=0,
        tiled=True,
    )
    hot_recv = lax.all_to_all(hot_send, "dp", split_axis=0, concat_axis=0, tiled=True)
    gathered = lax.all_gather(hot_recv, "ep", axis=0, tiled=True)
    own_slice = hot_weights[0]
    hot_sum = lax.psum_scatter(
        sliced_rows(gathered, own_slice), "ep", scatter_dimension=0, tiled=True
    )
    hot_back = lax.all_to_all(
        hot_sum.astype(jnp.bfloat16), "dp", split_axis=0, concat_axis=0, tiled=True
    )
    answers = jnp.concatenate(
        [cold_back.reshape(cold_size, model_width), hot_back.reshape(hot_size, model_width)], axis=0
    )
    positions = jnp.where(
        is_hot, cold_size + hot_index * most_rows + rank_ids, slot_ids * cold_cap + rank_ids
    )
    picked = jnp.take(answers, positions, axis=0)
    mixed = jnp.zeros((tok_rows, model_width), jnp.float32)
    for column in range(top_count):
        mixed = mixed + route_w[:, column, None] * picked[:, column].astype(jnp.float32)
    return mixed.astype(jnp.bfloat16)


def pin(array):
    return pltpu.with_memory_space_constraint(array, pltpu.VMEM)


NN = (((1,), (0,)), ((), ()))
NT = (((1,), (1,)), ((), ()))
TN = (((0,), (0,)), ((), ()))
STEP = 256
LANES = 128


def mm(a, b, dims=NN):
    return lax.dot_general(a, b, dims, preferred_element_type=jnp.float32)


def swish(gate, up):
    return (gate / (1.0 + jnp.exp(-gate)) * up).astype(jnp.bfloat16)


def message_kernel(hot_list_ref, slot_ref, tok_ref, ids_ref, gain_ref, out_ref, key_ref):
    width = tok_ref.shape[1]
    out_ref[:, :width] = tok_ref[...]
    bf16, f32 = jnp.bfloat16, jnp.float32
    gains = gain_ref[...]
    terms = [ids_ref[...].astype(f32)]
    for _ in range(3):
        term = gains.astype(bf16).astype(f32)
        terms.append(term)
        gains = gains - term
    stacked = jnp.concatenate(terms, axis=0).astype(bf16)
    shape = (stacked.shape[0], LANES)
    row, lane = (lax.broadcasted_iota(jnp.int32, shape, axis) for axis in (0, 1))
    place = jnp.where(row == lane, 1.0, 0.0).astype(bf16)
    out_ref[:, width:] = mm(stacked, place, TN).astype(bf16)
    along = lax.axis_index("dp")
    me = lax.axis_index("ep") * lax.axis_size("dp") + along
    my_cold, my_hot = jnp.int32(0), jnp.int32(0)
    for expert in range(slot_ref.shape[0]):
        my_cold = jnp.where(slot_ref[expert] == me, expert, my_cold)
    held = my_cold
    for place in range(hot_list_ref.shape[0]):
        my_cold = jnp.where(hot_list_ref[place] == held, -1, my_cold)
        my_hot = jnp.where(along == place, hot_list_ref[place], my_hot)
    row = lax.broadcasted_iota(jnp.int32, key_ref.shape, 0)
    key_ref[...] = jnp.where(row == 0, my_cold, my_hot).astype(f32)


def join_kernel(mine_ref, other_ref, out_ref):
    height = mine_ref.shape[0]
    out_ref[:height, :] = mine_ref[...]
    out_ref[height:, :] = other_ref[...]


def load_kernel(n, *refs):
    copies = []
    sems = refs[2 * n + 1]
    for index in range(n):
        src, dst = refs[index], refs[n + 1 + index]
        rows = src.shape[-2]
        parts = 2
        for part in range(parts):
            at = pl.ds(part * (rows // parts), rows // parts)
            lead = (0,) * (len(src.shape) - 2)
            if len(src.shape) == 4:
                for third in range(src.shape[1]):
                    copies.append((src.at[0, third, at], dst.at[0, third, at]))
            else:
                copies.append((src.at[lead + (at,)], dst.at[lead + (at,)]))
    started = []
    for number, (src, dst) in enumerate(copies):
        copy = pltpu.make_async_copy(src, dst, sems.at[number])
        copy.start()
        started.append(copy)
    for copy in started:
        copy.wait()


def routing(key_ref, meta, top, lanes):
    meta = meta.astype(jnp.float32)
    total = meta.shape[0]
    ids = meta[:, :top]
    gains = meta[:, top : 2 * top] + meta[:, 2 * top : 3 * top] + meta[:, 3 * top : 4 * top]
    is_cold = ids == key_ref[0:1, :top]
    is_hot = ids == key_ref[1:2, :top]
    cold_gain = jnp.sum(jnp.where(is_cold, gains, 0.0), axis=1, keepdims=True)
    hot_gain = jnp.sum(jnp.where(is_hot, gains, 0.0), axis=1, keepdims=True)
    mark = jnp.sum(jnp.where(is_cold, 1.0, 0.0), axis=1, keepdims=True)
    marks = jnp.broadcast_to(mark, (total, lanes))
    shape = (total, total)
    below = lax.broadcasted_iota(jnp.int32, shape, 0) > lax.broadcasted_iota(jnp.int32, shape, 1)
    rank = mm(jnp.where(below, 1.0, 0.0).astype(jnp.bfloat16), marks.astype(jnp.bfloat16))
    lane = lax.broadcasted_iota(jnp.int32, (total, lanes), 1).astype(jnp.float32)
    spread = jnp.where((marks > 0.5) & (rank == lane), 1.0, 0.0).astype(jnp.bfloat16)
    return cold_gain, hot_gain, spread


def load_rows(blocks, spans, x_ref):
    width, at, tails = x_ref.shape[1], 0, []
    for block, (first, size) in zip(blocks, spans):
        x_ref[at : at + size, :] = block[first : first + size, :width]
        tails.append(block[first : first + size, width : width + LANES])
        at += size
    return jnp.concatenate(tails, axis=0)


def weigh(hidden, packed_ref, spread, hot_ref, cold_gain, hot_gain, out_ref, first=0):
    width = out_ref.shape[1]
    rows = slice(first, first + hidden.shape[0])
    for start in range(0, width, STEP):
        at = slice(start, start + STEP)
        hot_part = mm(hidden, hot_ref[0, 2, :, at])
        cold_part = mm(spread, packed_ref[:, at])
        out_ref[rows, at] = (hot_gain * hot_part + cold_gain * cold_part).astype(out_ref.dtype)


def keep_gains(cold_gain, hot_gain, gain_ref):
    lane = lax.broadcasted_iota(jnp.int32, gain_ref.shape, 1)
    gain_ref[...] = jnp.where(lane == 0, cold_gain, hot_gain)


def early_kernel(spans, top, cap, key_ref, *refs):
    n = len(spans)
    hot_ref, hid_ref, pick_ref, spread_ref, gain_ref, x_ref = refs[n:]
    meta = load_rows(refs[:n], spans, x_ref)
    cold_gain, hot_gain, spread = routing(key_ref, meta, top, spread_ref.shape[1])
    spread_ref[...] = spread
    keep_gains(cold_gain, hot_gain, gain_ref)
    x = x_ref[...]
    hid_ref[...] = swish(mm(x, hot_ref[0, 0], NT), mm(x, hot_ref[0, 1], NT))
    pick_ref[...] = mm(spread[:, :cap], x, TN).astype(jnp.bfloat16)


def cold_expert(cold, gate_up_ref, down_ref, h_ref, packed_refs):
    units, width = down_ref.shape[1:]
    for start in range(0, units, STEP):
        gate = mm(cold, gate_up_ref[0, :, start : start + STEP])
        up = mm(cold, gate_up_ref[0, :, units + start : units + start + STEP])
        h_ref[:, start : start + STEP] = swish(gate, up)
    cold_hidden = h_ref[...]
    for start in range(0, width, STEP):
        at = slice(start, start + STEP)
        packed, end = mm(cold_hidden, down_ref[0, :, at]).astype(jnp.bfloat16), 0
        for packed_ref in packed_refs:
            packed_ref[:, at] = packed[end : end + packed_ref.shape[0]]
            end += packed_ref.shape[0]


def first_kernel(spans, top, cap, key_ref, *refs):
    n = len(spans)
    (gate_up_ref, down_ref, hot_ref), rest = refs[n : n + 3], refs[n + 3 :]
    hid_ref, packed_ref, spread_ref, gain_ref, x_ref, h_ref = rest
    meta = load_rows(refs[:n], spans, x_ref)
    cold_gain, hot_gain, spread = routing(key_ref, meta, top, spread_ref.shape[1])
    spread_ref[...] = spread
    keep_gains(cold_gain, hot_gain, gain_ref)
    x = x_ref[...]
    hid_ref[...] = swish(mm(x, hot_ref[0, 0], NT), mm(x, hot_ref[0, 1], NT))
    cold = mm(spread[:, :cap], x, TN).astype(jnp.bfloat16)
    cold_expert(cold, gate_up_ref, down_ref, h_ref, (packed_ref,))


def late_kernel(spans, top, cap, skip, key_ref, *refs):
    n = len(spans)
    (pick_ref, gate_up_ref, down_ref, hot_ref), rest = refs[n : n + 4], refs[n + 4 :]
    sib_ref, hid_ref, *packed_refs = rest[:4]
    spread_ref, gain_ref, x_ref, c_ref, h_ref = rest[4:]
    width = x_ref.shape[1]
    meta = load_rows(refs[:n], spans, x_ref)
    cold_gain, hot_gain, spread = routing(key_ref, meta, top, spread_ref.shape[1])
    spread_ref[...] = spread
    keep_gains(cold_gain, hot_gain, gain_ref)
    spread = spread[:, :cap]
    x = x_ref[...]
    n_picked = pick_ref.shape[0]
    c_ref[:n_picked, :] = pick_ref[...]
    c_ref[n_picked:, :] = mm(spread, x, TN).astype(jnp.bfloat16)
    cold_expert(c_ref[...], gate_up_ref, down_ref, h_ref, packed_refs)
    hidden = swish(mm(x, hot_ref[0, 0], NT), mm(x, hot_ref[0, 1], NT))
    hid_ref[...] = hidden
    weigh(
        hidden[skip:], packed_refs[1], spread[skip:], hot_ref, cold_gain[skip:], hot_gain[skip:], sib_ref
    )


def result_kernel(n_groups, jobs, hot_ref, *refs):
    outs = refs[4 * n_groups :]
    for group, first, size, out, place in jobs:
        hid_ref, packed_ref, spread_ref, gain_ref = refs[4 * group : 4 * group + 4]
        at = slice(first, first + size)
        weigh(
            hid_ref[at, :],
            packed_ref,
            spread_ref[at, : packed_ref.shape[0]],
            hot_ref,
            gain_ref[at, 0:1],
            gain_ref[at, 1:2],
            outs[out],
            place,
        )


def run_kernel(kernel, operands, outs, scratch, flops, moved, limit=12):
    vmem = pl.BlockSpec(memory_space=pltpu.VMEM)
    return pl.pallas_call(
        kernel,
        out_shape=[pltpu.VMEM(shape, dtype) for shape, dtype in outs],
        in_specs=[vmem] * len(operands),
        out_specs=[vmem] * len(outs),
        scratch_shapes=[pltpu.VMEM(shape, dtype) for shape, dtype in scratch],
        compiler_params=pltpu.CompilerParams(vmem_limit_bytes=limit * 2**20),
        cost_estimate=pl.CostEstimate(flops=flops, bytes_accessed=moved, transcendentals=0),
    )(*[pin(a) for a in operands])


def load_weights(weights, after):
    n = len(weights)
    hbm = lambda a: pltpu.with_memory_space_constraint(a, pltpu.HBM)
    return pl.pallas_call(
        functools.partial(load_kernel, n),
        out_shape=[pltpu.VMEM(w.shape, w.dtype) for w in weights],
        in_specs=[pl.BlockSpec(memory_space=pltpu.HBM)] * n + [pl.BlockSpec(memory_space=pl.ANY)],
        out_specs=[pl.BlockSpec(memory_space=pltpu.VMEM)] * n,
        scratch_shapes=[pltpu.SemaphoreType.DMA((4 * n + 8,))],
        compiler_params=pltpu.CompilerParams(vmem_limit_bytes=2**20),
        cost_estimate=pl.CostEstimate(
            flops=0, bytes_accessed=sum(w.size * 2 for w in weights), transcendentals=0
        ),
    )(*[hbm(w) for w in weights], after)


def make_message(hot_list, slot_of, tokens, ids, gains):
    rows, width = tokens.shape
    vmem, smem = pl.BlockSpec(memory_space=pltpu.VMEM), pl.BlockSpec(memory_space=pltpu.SMEM)
    hbm = lambda a: pltpu.with_memory_space_constraint(a, pltpu.HBM)
    return pl.pallas_call(
        message_kernel,
        out_shape=[
            pltpu.VMEM((rows, width + LANES), tokens.dtype),
            pltpu.VMEM((8, LANES), jnp.float32),
        ],
        in_specs=[smem] * 2 + [vmem] * 3,
        out_specs=[vmem] * 2,
        compiler_params=pltpu.CompilerParams(vmem_limit_bytes=2**21),
    )(*[hbm(a) for a in (hot_list, slot_of, tokens, ids, gains)])


def ring_perms(n_dp):
    chips = [(0, z) for z in range(n_dp)] + [(1, z) for z in reversed(range(n_dp))]
    size = len(chips)

    def device(place, core):
        x, z = chips[place % size]
        return (2 * x + core) * n_dp + z

    def hop(by, cross):
        return [
            (device(i, core), device(i + (-by if core else by), core ^ cross))
            for i in range(size)
            for core in range(2)
        ]

    swap = [(device(i, core), device(i, 1 - core)) for i in range(size) for core in range(2)]
    return hop, swap


def dense_body(tokens, expert_ids, route_w, hot_list, slot_of, cold_gate_up, cold_down, hot_weights):
    tok_rows, width = tokens.shape
    top = expert_ids.shape[1]
    n_hot, n_exp = hot_list.shape[0], slot_of.shape[0]
    n_dp = lax.axis_size("dp")
    units, hot_units = cold_down.shape[1], hot_weights.shape[3]
    cold_cap = -(-(tok_rows * top - n_hot * tok_rows) // (n_exp - n_hot))
    f32, bf16 = jnp.float32, jnp.bfloat16
    hop, swap_pairs = ring_perms(n_dp)
    axes = ("ep", "dp")
    move = lambda a, by: lax.ppermute(a, axes, hop(by, 0))
    cross = lambda a, by: lax.ppermute(a, axes, hop(by, 1))
    swap = lambda a: lax.ppermute(a, axes, swap_pairs)
    tie = lambda *arrays: lax.optimization_barrier(arrays)

    mine, key = make_message(hot_list, slot_of, tokens, expert_ids.T, route_w.T)
    (message,) = run_kernel(
        join_kernel, (mine, swap(mine)), [((2 * tok_rows, mine.shape[1]), bf16)], [], 0, 4 * mine.size, 2
    )
    weights = (cold_gate_up, cold_down, jnp.swapaxes(hot_weights, 2, 3))
    gate_up, down, hot = load_weights(weights, message)

    two = move(message, 2)
    later, hot = tie(message, hot)
    one = move(later, 1)
    two, hot = tie(two, hot)
    four, three = move(two[:tok_rows], 2), move(two, 1)

    sib_two = swap(two)
    whole, half, rest = (0, 2 * tok_rows), (0, tok_rows), (tok_rows, tok_rows)
    pad = lambda n: -(-n * cold_cap // 16) * 16
    lanes = lambda cap: -(-cap // LANES) * LANES

    def facts(spans):
        rows = sum(size for _, size in spans)
        cap = pad(rows // tok_rows)
        kept = [((rows, lanes(cap)), bf16), ((rows, LANES), f32)]
        return rows, cap, kept

    def early(blocks, spans):
        rows, cap, kept = facts(spans)
        return run_kernel(
            functools.partial(early_kernel, spans, top, cap),
            (key, *blocks, hot),
            [((rows, hot_units), bf16), ((cap, width), bf16), *kept],
            [((rows, width), bf16)],
            2 * rows * width * (2 * hot_units + cap),
            4 * rows * width,
        )

    spans = (whole, half, whole, rest, whole)
    rows, cap_a, kept = facts(spans)
    a_rows = run_kernel(
        functools.partial(first_kernel, spans, top, cap_a),
        (key, two, message, sib_two, message, one, gate_up, down, hot),
        [((rows, hot_units), bf16), ((cap_a, width), bf16), *kept],
        [((rows, width), bf16), ((cap_a, units), bf16)],
        2 * cap_a * 3 * units * width,
        4 * rows * width,
    )
    def results(groups, jobs, outs):
        size = sum(job[2] for job in jobs)
        return run_kernel(
            functools.partial(result_kernel, len(groups), jobs),
            (hot, *[a for group in groups for a in group]),
            outs,
            [],
            2 * size * width * (hot_units + cap_a),
            4 * size * width,
        )

    r = tok_rows
    back_a, mine = results(
        (a_rows,),
        (
            (0, 3 * r, 3 * r, 0, 0),
            (0, 0, 2 * r, 1, 0),
            (0, 6 * r, 2 * r, 1, 2 * r),
            (0, 2 * r, r, 1, 4 * r),
        ),
        [((3 * r, width), bf16), ((5 * r, width), f32)],
    )
    four, three, one, mine = tie(four, three, one, mine)
    sib_one, sib_four, sib_three = swap(one), swap(four), swap(three)
    hid_b, pick_b, *kept_b = early((four, three), (half, whole))
    spans = (whole, half, whole)
    rows, cap, kept = facts(spans)
    cap_b, skip = pick_b.shape[0], 2 * tok_rows
    back_late, hid_c, packed_b, packed_c, *kept_c = run_kernel(
        functools.partial(late_kernel, spans, top, cap, skip),
        (key, sib_one, sib_four, sib_three, pick_b, gate_up, down, hot),
        [
            ((rows - skip, width), bf16),
            ((rows, hot_units), bf16),
            ((cap_b, width), bf16),
            ((cap, width), bf16),
            *kept,
        ],
        [((rows, width), bf16), ((cap_b + cap, width), bf16), ((cap_b + cap, units), bf16)],
        2 * (cap_b + cap) * 3 * units * width,
        4 * rows * width,
    )
    b_rows = (hid_b, packed_b, *kept_b)
    c_rows = (hid_c, packed_c, *kept_c)
    low = lambda a: a.astype(bf16)
    from_late = swap(back_late)
    back_one, mine_late = results(
        (b_rows, c_rows),
        ((1, 0, 2 * r, 0, 0), (0, 0, 3 * r, 1, 0)),
        [((2 * r, width), bf16), ((3 * r, width), f32)],
    )
    from_a, from_one = swap(back_a), swap(back_one)
    join = lambda a, b: low(a + b.astype(f32))
    fourth, third = join(mine_late[:r], from_late[:r]), join(mine_late[r:], from_late[r:])
    fourth, third = move(fourth, -2), move(third, -1)
    far_sum = mine[: 2 * r] + from_a[: 2 * r].astype(f32)
    one_sum = mine[2 * r : 4 * r] + from_one.astype(f32)
    own_sum = mine[4 * r :] + from_a[2 * r :].astype(f32)
    fourth, nearest = tie(fourth, low(one_sum))
    close = move(nearest, -1)
    far = tie(low(far_sum[:r] + third[:r].astype(f32) + fourth.astype(f32)), join(far_sum[r:], third[r:]))
    parts = (close[:tok_rows], swap(close[tok_rows:]), move(far[0], -2), cross(far[1], -2))
    return low(sum((a.astype(f32) for a in parts), own_sum))


def body(tokens, expert_ids, *rest):
    hot_list, slot_of = rest[1], rest[2]
    every_row_hot = 2 * expert_ids.shape[1] == slot_of.shape[0]
    two_columns = lax.axis_size("ep") == 4 and lax.axis_size("dp") == 4
    chosen = dense_body if every_row_hot and two_columns else routed_body
    return chosen(tokens, expert_ids, *rest)


def solution(mesh):
    in_specs = (
        P(("groups", "ep", "dp"), None),
        P(("groups", "ep", "dp"), None),
        P(("groups", "ep", "dp"), None),
        P("groups"),
        P(),
        P(("ep", "dp"), None, None),
        P(("ep", "dp"), None, None),
        P("dp", None, None, "ep"),
    )
    out_specs = P(("groups", "ep", "dp"), None)
    return jax.shard_map(body, mesh=mesh, in_specs=in_specs, out_specs=out_specs, check_vma=False)
```
